32 devices in a mesh: row: 4 (over y, x), col: 8 (over z, core).
Axes of the slice: x: 2, y: 2, z: 4, core: 2. Of those that a mesh axis runs over, the one named last changes fastest.
Arguments:
- field: float32 [2, 1024, 4096], P(None, 'row', 'col'), may hold values from -4 to 4
- states: float32 [16, 64, 512], P('row', 'col'), may hold values from -1 to 1
- input_weight: bfloat16 [20736, 512], P('col'), may hold values from -0.0390625 to 0.0390625
- recurrent_weight: bfloat16 [512, 512], replicated, may hold values from -0.25 to 0.25
- bias: float32 [512], replicated, may hold values from -3 to 3
- output_weight: bfloat16 [512, 8192], P(None, 'col'), may hold values from -0.25 to 0.25
- model_gain: float32 [2, 64, 64], replicated, may hold values from 0.5 to 1.5
Outputs:
- prediction: float32 [2, 1024, 4096], P(None, 'row', 'col')
- fresh_states: float32 [16, 64, 512], P('row', 'col')
The draws below stay inside these ranges and needn't reach their ends.
All inputs are finite; a program needn't handle non-finite values.
Results may differ from the reference program's by a relative error of at most 0.0033.
Values may be sent and summed in bfloat16 or wider, within the bound.
No kernel may reach another device: no remote copies, remote signals or barrier semaphores. Data moves between devices by JAX's collectives and lax.ppermute only.
A program may use at most 64 MiB of HBM per device.

```python
import jax
import jax.numpy as jnp
from jax import lax

CORE = 64
MARGIN = 4
NODES = 512
PATCH = 72
FEAT = 20736
NR = 1024
NC = 4096
BLK_ROWS = 16
BLK_COLS = 64


def level_of(rng, extent, shards, smallest, largest):
    def one(axis_at, shards_of):
        steps = jax.random.uniform(jax.random.fold_in(jax.random.fold_in(rng, 6), axis_at), (shards_of,), jnp.float32, smallest / len(shards), largest / len(shards))
        return jnp.repeat(jnp.exp(steps), extent[axis_at] // shards_of).reshape((-1,) + (1,) * (len(extent) - axis_at - 1))

    level = one(*shards[0])
    for cut in shards[1:]:
        level = level * one(*cut)
    return level


def normal_values(rng, dims, deviation, most, split=(), kind=jnp.bfloat16):
    array = jax.random.normal(rng, dims, jnp.float32) * deviation
    if len(split) > 0:
        array = level_of(rng, dims, split, -0.22, 0.18) * array
    return jnp.clip(array, min=-most, max=most).astype(kind)


def setup_inputs(seed: int = 0) -> dict:
    streams_of = jax.random.split(jax.random.key(seed), 8)
    field = normal_values(streams_of[0], (2, NR, NC), 0.6, 4.0, ((1, 4), (2, 8)), jnp.float32)
    states = jnp.clip(jax.random.uniform(streams_of[1], (BLK_ROWS, BLK_COLS, NODES), jnp.float32, -1.0, 1.0) * level_of(streams_of[1], (BLK_ROWS, BLK_COLS, NODES), ((0, 4), (1, 8)), -0.4, 0.0), -1.0, 1.0)
    input_weight = normal_values(streams_of[2], (FEAT, NODES), FEAT ** -0.5, 0.0390625, ((0, 8),))
    recurrent_weight = normal_values(streams_of[3], (NODES, NODES), NODES ** -0.5, 0.25)
    bias = normal_values(streams_of[4], (NODES,), 0.5, 3.0, (), jnp.float32)
    output_weight = normal_values(streams_of[5], (NODES, 2 * CORE * CORE), NODES ** -0.5, 0.25, ((1, 8),))
    model_gain = jnp.clip(1.0 + 0.1 * jax.random.normal(streams_of[6], (2, CORE, CORE), jnp.float32), 0.5, 1.5)
    return dict(field=field, states=states, input_weight=input_weight, recurrent_weight=recurrent_weight, bias=bias, output_weight=output_weight, model_gain=model_gain)


dispersion = 2.0
nonlinear = -0.7
time_step = 0.1


def reaction(center, spread):
    real_part = center[0]
    imag_part = center[1]
    modulus = real_part * real_part + imag_part * imag_part
    first = real_part + spread[0] - dispersion * spread[1] - modulus * (real_part - nonlinear * imag_part)
    second = imag_part + spread[1] + dispersion * spread[0] - modulus * (imag_part + nonlinear * real_part)
    return jnp.stack([first, second])


def tendency(field):
    spread = jnp.roll(field, 1, 1) + jnp.roll(field, -1, 1) + jnp.roll(field, 1, 2) + jnp.roll(field, -1, 2) - 4.0 * field
    return reaction(field, spread)


def reference(field, states, input_weight, recurrent_weight, bias, output_weight, model_gain):
    slope_one = tendency(field)
    slope_two = tendency(field + 0.5 * time_step * slope_one)
    slope_three = tendency(field + 0.5 * time_step * slope_two)
    slope_four = tendency(field + time_step * slope_three)
    model = field + time_step / 6.0 * (slope_one + 2.0 * slope_two + 2.0 * slope_three + slope_four)
    both = jnp.concatenate([field, model], 0)
    padded = jnp.pad(both, ((0, 0), (MARGIN, MARGIN), (MARGIN, MARGIN)), mode="wrap")
    starts = jnp.arange(BLK_COLS, dtype=jnp.int32) * CORE

    def one_row(index):
        slab = lax.dynamic_slice_in_dim(padded, (index * CORE).astype(jnp.int32), PATCH, 1)

        def one_patch(start):
            return lax.dynamic_slice_in_dim(slab, start.astype(jnp.int32), PATCH, 2)

        inputs = jax.vmap(one_patch)(starts).reshape(BLK_COLS, FEAT).astype(jnp.bfloat16)
        previous = lax.dynamic_index_in_dim(states, index, 0, keepdims=False).astype(jnp.bfloat16)
        drive = jnp.dot(inputs, input_weight, preferred_element_type=jnp.float32)
        recur = jnp.dot(previous, recurrent_weight, preferred_element_type=jnp.float32)
        fresh = jnp.tanh(drive + recur + bias)
        readout = jnp.dot(fresh.astype(jnp.bfloat16), output_weight, preferred_element_type=jnp.float32)
        return fresh, readout

    fresh_states, readout = lax.map(one_row, jnp.arange(BLK_ROWS, dtype=jnp.int32))
    placed = readout.reshape(BLK_ROWS, BLK_COLS, 2, CORE, CORE).transpose(2, 0, 3, 1, 4).reshape(2, NR, NC)
    gained = (model.reshape(2, BLK_ROWS, CORE, BLK_COLS, CORE) * model_gain[:, None, :, None, :]).reshape(2, NR, NC)
    prediction = gained + placed
    return prediction, fresh_states
```

```python
import functools

import jax
import jax.numpy as jnp
from jax import lax
from jax.experimental import pallas as pl
from jax.experimental.pallas import tpu as pltpu
from jax.sharding import PartitionSpec as P

CORE = 64
MARGIN = 4
NODES = 512
PATCH = 72
LANES = 128
STAGES = 4
GROUP = 8
REACH = MARGIN + STAGES
WINDOW = CORE + 2 * REACH

dispersion = 2.0
nonlinear = -0.7
time_step = 0.1

bf16 = jnp.bfloat16
f32 = jnp.float32
VMEM = pl.BlockSpec(memory_space=pltpu.VMEM)
SMEM = pl.BlockSpec(memory_space=pltpu.SMEM)


def call(kernel, outs, operands, scratch=(), megabytes=32, name=None):
    return pl.pallas_call(
        kernel,
        out_shape=tuple(jax.ShapeDtypeStruct(*out) for out in outs),
        in_specs=[SMEM] + [VMEM] * (len(operands) - 1),
        out_specs=tuple(VMEM for _ in outs),
        scratch_shapes=list(scratch),
        compiler_params=pltpu.CompilerParams(vmem_limit_bytes=megabytes * 2**20),
        name=name,
    )(*operands)


def tendency(real_part, imag_part):
    def spread(values):
        rows, cols = values.shape
        return (
            pltpu.roll(values, 1, 0)
            + pltpu.roll(values, rows - 1, 0)
            + pltpu.roll(values, 1, 1)
            + pltpu.roll(values, cols - 1, 1)
            - 4.0 * values
        )

    real_spread = spread(real_part)
    imag_spread = spread(imag_part)
    modulus = real_part * real_part + imag_part * imag_part
    first = (
        real_part
        + real_spread
        - dispersion * imag_spread
        - modulus * (real_part - nonlinear * imag_part)
    )
    second = (
        imag_part
        + imag_spread
        + dispersion * real_spread
        - modulus * (imag_part + nonlinear * real_part)
    )
    return first, second


def forecast(start):
    slope = tendency(*start)
    total = slope
    for ahead, weight in ((0.5, 2.0), (0.5, 2.0), (1.0, 1.0)):
        at = tuple(s + ahead * time_step * k for s, k in zip(start, slope))
        slope = tendency(*at)
        total = tuple(t + weight * k for t, k in zip(total, slope))
    return tuple(s + time_step / 6.0 * t for s, t in zip(start, total))


def aligned(value):
    return pl.multiple_of(value, GROUP)


def both_cores(half, own, other):
    low = jnp.where(half == 0, own, other)
    high = jnp.where(half == 0, other, own)
    return low, high


def tile_of(values, tile):
    return values[:, tile * LANES : (tile + 1) * LANES]


def write_lines(lines_ref, channel, tile, values):
    depth = lines_ref.shape[2]
    for part in range(PATCH // depth):
        at = MARGIN + part * depth
        lines_ref[channel * (PATCH // depth) + part, tile] = values[at : at + depth].astype(bf16)


def send_lines(place_ref, lines_ref, message_refs):
    pairs = len(message_refs)
    for ahead, message_ref in enumerate(message_refs):
        message_ref[...] = lines_ref[lax.rem(place_ref[1] + ahead, pairs)]


def inner_kernel(place_ref, field_ref, other_ref, *refs):
    message_refs, (model_ref, lines_ref) = refs[:-2], refs[-2:]
    half = place_ref[0]
    at = aligned((other_ref.shape[1] - WINDOW) * (1 - half))
    at_own = aligned(at + half * (field_ref.shape[1] - other_ref.shape[1]))
    start = []
    for channel in range(2):
        own = field_ref[channel, pl.ds(at_own, WINDOW), :]
        other = other_ref[channel, pl.ds(at, WINDOW), :]
        start.append(jnp.concatenate(both_cores(half, own, other), 1))
    model = forecast(start)
    tiles = start[0].shape[1] // LANES
    for channel, values in enumerate(tuple(start) + model):
        for tile in range(1, tiles - 1):
            write_lines(lines_ref, channel, tile - 1, tile_of(values, tile))
    for channel in range(2):
        model_ref[channel] = model[channel][REACH : REACH + CORE]
    send_lines(place_ref, lines_ref, message_refs)


def outer_kernel(place_ref, field_ref, other_ref, side_ref, ends_ref, inner_ref, gain_ref, *refs):
    message_refs, (same_ref, away_ref, lines_ref, window_ref) = refs[:-4], refs[-4:]
    half = place_ref[0]
    width = field_ref.shape[2]
    rows = other_ref.shape[1]
    tiles = 2 * width // LANES
    shift = half * (field_ref.shape[1] - rows)
    at = aligned((rows - WINDOW) * (1 - half))
    start = []
    for channel in range(2):
        own = field_ref[channel, pl.ds(aligned(at + shift), WINDOW), :]
        other = other_ref[channel, pl.ds(at, WINDOW), :]
        low, high = both_cores(half, own, other)
        side = side_ref[channel, pl.ds(at, WINDOW), :]
        start.append(jnp.concatenate([high[:, width - 2 * LANES :], side, low[:, : 2 * LANES]], 1))
    model = forecast(start)
    for channel, values in enumerate(tuple(start) + model):
        write_lines(lines_ref, channel, 0, tile_of(values, 3))
        write_lines(lines_ref, channel, 1, tile_of(values, 1))
    first = [values[REACH : REACH + CORE] for values in model]

    length = WINDOW - REACH
    at = aligned((rows - length) * half)
    start = []
    for channel in range(2):
        own = field_ref[channel, pl.ds(aligned(at + shift), length), :]
        other = other_ref[channel, pl.ds(at, length), :]
        side = side_ref[channel, pl.ds(at, length), :]
        cells = jnp.concatenate(both_cores(half, own, other) + (side,), 1)
        window_ref[channel, pl.ds(aligned(REACH * (1 - half)), length), :] = cells
        window_ref[channel, pl.ds(aligned(length * half), REACH), :] = ends_ref[channel]
        start.append(window_ref[channel])
    model = forecast(start)
    for channel, values in enumerate(tuple(start) + model):
        for tile in range(tiles):
            write_lines(lines_ref, channel, 2 + tile, tile_of(values, tile))
    send_lines(place_ref, lines_ref, message_refs)

    for channel in range(2):
        gain = gain_ref[channel]
        second = model[channel][REACH : REACH + CORE]
        for tile in range(tiles // 2):
            lanes = slice(tile * LANES, (tile + 1) * LANES)
            far = slice(width + tile * LANES, width + (tile + 1) * LANES)
            low = tile_of(first[channel], 3) if tile == 0 else inner_ref[channel, :, lanes]
            high = tile_of(first[channel], 1) if tile == tiles // 2 - 1 else inner_ref[channel, :, far]
            for row, (left, right) in enumerate(((low, high), (second[:, lanes], second[:, far]))):
                same_ref[channel, row, :, lanes] = gain * jnp.where(half == 0, left, right)
                away_ref[channel, row, :, lanes] = gain * jnp.where(half == 0, right, left)


def drive_kernel(pairs, place_ref, *refs):
    inner_refs, outer_refs, weight_refs = refs[:pairs], refs[pairs : 2 * pairs], refs[2 * pairs : 2 * pairs + 2]
    out_refs, (cells_ref, left_ref) = refs[2 * pairs + 2 : -2], refs[-2:]
    tiles, depth = outer_refs[0].shape[0] - 2, outer_refs[0].shape[1]
    total = pairs * tiles
    for pair in range(pairs):
        for row in range(2):
            for tile in range(tiles):
                if row == 1:
                    values = outer_refs[pair][2 + tile]
                elif tile == 0 or tile == tiles - 1:
                    values = outer_refs[pair][0 if tile == 0 else 1]
                else:
                    values = inner_refs[pair][tile - 1]
                at = (row * total + pair * tiles + tile) * depth
                cells_ref[at : at + depth, :] = values.astype(f32)
    lane = lax.broadcasted_iota(jnp.int32, (total, LANES), 1)
    half = place_ref[0]
    lines = depth // 2
    width = lines * PATCH
    sums = None
    for which in range(2):
        begin = lines * (half if which == 0 else 1 - half)
        for row in range(2):
            held = [None, None]
            for line in range(lines):
                own = cells_ref[pl.ds(row * total * depth + begin + line, total, stride=depth), :]
                before = pltpu.roll(own, 1, 0)
                after = pltpu.roll(own, total - 1, 0)
                even = jnp.where(lane >= LANES - MARGIN, before, own)
                odd = jnp.where(lane < MARGIN, after, own)
                first = line * PATCH
                offset = first % LANES
                lanes = slice(first - offset, first - offset + LANES)
                for parity, (values, shift) in enumerate(((even, MARGIN), (odd, MARGIN + CORE))):
                    at = (parity * 2 + row) * total
                    moved = pltpu.roll(values, (first + shift) % LANES, 1)
                    current = moved if offset == 0 else jnp.where(lane >= offset, moved, held[parity])
                    if offset + PATCH >= LANES or line == lines - 1:
                        left_ref[at : at + total, lanes] = current.astype(bf16)
                        if line == lines - 1 and offset + PATCH > LANES:
                            more = slice(lanes.stop, lanes.stop + LANES)
                            left_ref[at : at + total, more] = moved.astype(bf16)
                        current = moved
                    held[parity] = current
        term = jnp.dot(left_ref[:, :width], weight_refs[which][...], preferred_element_type=f32)
        sums = term if sums is None else sums + term
    for pair, out_ref in enumerate(out_refs):
        pieces = []
        for of in (pair, (pair + pairs // 2) % pairs):
            for row in range(2):
                for parity in range(2):
                    at = (parity * 2 + row) * total + of * tiles
                    pieces.append(sums[at : at + tiles])
        out_ref[...] = jnp.concatenate(pieces, 0).astype(bf16)


def halves(half, first, second):
    rows = first.shape[0]
    row = lax.broadcasted_iota(jnp.int32, first.shape, 0)
    low = jnp.where(row < rows // 2, first, pltpu.roll(second, rows // 2, 0))
    high = jnp.where(row < rows // 2, pltpu.roll(first, rows // 2, 0), second)
    return jnp.where(half == 0, low, high), jnp.where(half == 0, high, low)


def readout_kernel(pairs, slices, place_ref, *refs):
    parts, recur_ref, weights = refs[:pairs], refs[pairs], refs[pairs + 1 : pairs + 1 + slices]
    fresh_same, fresh_away, own_same, own_away, far_same, far_away = refs[pairs + 1 + slices :]
    half = place_ref[0]
    total = recur_ref[...]
    for part in parts:
        total = total + part[...].astype(f32)
    fresh = jnp.tanh(total)
    tiles = fresh.shape[0] // 8
    for row in range(2):
        at = row * 2 * tiles
        same, away = halves(half, fresh[at : at + tiles], fresh[at + tiles : at + 2 * tiles])
        fresh_same[row] = same
        fresh_away[row] = away
    readin = fresh.astype(bf16)
    lane = lax.broadcasted_iota(jnp.int32, (tiles, LANES), 1)
    for index, weight in enumerate(weights):
        products = jnp.dot(readin, weight[...], preferred_element_type=f32)
        lines = products.shape[1] // CORE
        begin = lax.bitwise_xor(place_ref[2], index) * lines
        for tile in range(products.shape[1] // LANES):
            values = tile_of(products, tile)
            for of, (same_ref, away_ref) in enumerate(((own_same, own_away), (far_same, far_away))):
                pair = []
                for row in range(2):
                    at = (of * 2 + row) * 2 * tiles
                    low, high = values[at : at + tiles], values[at + tiles : at + 2 * tiles]
                    pair.append(
                        (
                            jnp.where(lane < CORE, low, pltpu.roll(high, CORE, 1)),
                            jnp.where(lane < CORE, pltpu.roll(low, CORE, 1), high),
                        )
                    )
                for line in range(2):
                    same, away = halves(half, pair[0][line], pair[1][line])
                    same_ref[begin + 2 * tile + line] = same.astype(bf16)
                    away_ref[begin + 2 * tile + line] = away.astype(bf16)


def final_kernel(
    place_ref,
    own_same,
    own_away,
    far_same,
    far_away,
    gained_same,
    gained_away,
    fresh_same,
    fresh_away,
    out_ref,
    states_ref,
    cells_ref,
):
    half = place_ref[0]
    side = place_ref[3]
    tiles = out_ref.shape[2] // LANES
    block_rows = out_ref.shape[1] // CORE
    rows = 2 * tiles
    for away, (own, far, gained, fresh) in enumerate(
        ((own_same, far_same, gained_same, fresh_same), (own_away, far_away, gained_away, fresh_away))
    ):
        of = half if away == 0 else 1 - half
        places = (block_rows // 2 - 1 + of, (block_rows - 1) * of)
        for opposite, values in enumerate((own, far)):
            channel = side if opposite == 0 else 1 - side
            cells_ref[...] = values[...].astype(f32).reshape(CORE * rows, LANES)
            for row in range(2):
                for tile in range(tiles):
                    lanes = slice(tile * LANES, (tile + 1) * LANES)
                    placed = cells_ref[pl.ds(row * tiles + tile, CORE, stride=rows), :]
                    at = pl.multiple_of(places[row] * CORE, CORE)
                    out_ref[channel, pl.ds(at, CORE), lanes] = gained[channel, row, :, lanes] + placed
        for row in range(2):
            for column in range(2 * tiles):
                at = (column % 2) * tiles + column // 2
                states_ref[places[row], column : column + 1, :] = fresh[row, at : at + 1, :]


def local(field, states, input_weight, recurrent_weight, bias, output_weight, model_gain):
    height, width = field.shape[1:]
    sections = lax.axis_size("col")
    bands = lax.axis_size("row")
    pairs = sections // 2
    block_rows = height // CORE
    tiles = width // LANES
    depth = 4 * PATCH // pairs
    slices = sections // 2
    rows = height // 2 + REACH
    column = lax.axis_index("col")
    half = column % 2
    place = jnp.stack([half, column // 2, column % slices, column // slices])

    def across(values):
        return lax.ppermute(values, "col", [(i, i ^ 1) for i in range(sections)])

    def along(values, ahead):
        if ahead % pairs == 0:
            return values
        return lax.ppermute(values, "col", [(i, (i + 2 * ahead) % sections) for i in range(sections)])

    def own_rows(begin, count):
        return lax.dynamic_slice_in_dim(field, begin, count, 1)

    beyond = height - rows
    other = across(own_rows((1 - half) * beyond, rows))

    mine = own_rows(half * beyond, rows)
    first = half == 0
    left_edge = jnp.where(first, mine[:, :, :STAGES], other[:, :, :STAGES])
    right_edge = jnp.where(first, other[:, :, width - STAGES :], mine[:, :, width - STAGES :])
    after = along(left_edge, -1)
    before = along(right_edge, 1)

    inner = call(
        inner_kernel,
        [((2 * tiles - 2, depth, LANES), bf16)] * pairs + [((2, CORE, 2 * width), f32)],
        (place, field, other),
        [pltpu.VMEM((pairs, 2 * tiles - 2, depth, LANES), bf16)],
        name="inner_model",
    )
    inner_messages, inner_model = inner[:pairs], inner[pairs]
    inner_patches = [along(inner_messages[-ahead % pairs], -ahead) for ahead in range(pairs)]

    side = jnp.concatenate([after, jnp.zeros((2, rows, LANES - 2 * STAGES), f32), before], 2)
    edge = half * (rows - REACH)
    near = own_rows(half * (height - REACH), REACH)
    far = lax.dynamic_slice_in_dim(other, edge, REACH, 1)
    ends = jnp.concatenate(
        [jnp.where(first, near, far), jnp.where(first, far, near), lax.dynamic_slice_in_dim(side, edge, REACH, 1)], 2
    )
    pattern = []
    for band in range(bands):
        for item in range(0, sections, 2):
            pattern.append((band * sections + item, (band - 1) % bands * sections + item + 1))
            pattern.append((band * sections + item + 1, (band + 1) % bands * sections + item))
    ends = lax.ppermute(ends, ("row", "col"), pattern)

    outer = call(
        outer_kernel,
        [((2 * tiles + 2, depth, LANES), bf16)] * pairs + [((2, 2, CORE, width), f32)] * 2,
        (place, field, other, side, ends, inner_model, jnp.concatenate([model_gain, model_gain], 2)),
        [
            pltpu.VMEM((pairs, 2 * tiles + 2, depth, LANES), bf16),
            pltpu.VMEM((2, WINDOW, 2 * width + LANES), f32),
        ],
        name="outer_model",
    )
    outer_messages, (gained_same, gained_away) = outer[:pairs], outer[pairs:]
    outer_patches = [along(outer_messages[-ahead % pairs], -ahead) for ahead in range(pairs)]
    gained_away = across(gained_away)

    weight_other = across(input_weight)
    readout_weights = [output_weight]
    for index in range(1, slices):
        if index % 2:
            readout_weights.append(across(readout_weights[index - 1]))
        else:
            pattern = [(i, i ^ index) for i in range(sections)]
            readout_weights.append(lax.ppermute(output_weight, "col", pattern))
    previous = states.astype(bf16).reshape(2, block_rows // 2, tiles, 2, NODES)
    kept = lax.dynamic_index_in_dim(previous, half, 0, keepdims=False)
    got = across(lax.dynamic_index_in_dim(previous, 1 - half, 0, keepdims=False))
    chip = jnp.stack([jnp.where(first, kept, got), jnp.where(first, got, kept)])
    chip = jnp.where(first, chip[:, ::-1], chip)
    chip = chip.transpose(1, 3, 0, 2, 4).reshape(-1, NODES)
    recur = jnp.dot(
        jnp.concatenate([chip, along(chip, pairs // 2)], 0), recurrent_weight, preferred_element_type=f32
    ) + bias

    total = pairs * 2 * tiles
    parts = call(
        functools.partial(drive_kernel, pairs),
        [((8 * 2 * tiles, NODES), bf16)] * pairs,
        (place, *inner_patches, *outer_patches, input_weight, weight_other),
        [
            pltpu.VMEM((2 * total * depth, LANES), f32),
            pltpu.VMEM((4 * total, -(-depth // 2 * PATCH // LANES) * LANES), bf16),
        ],
        megabytes=40,
        name="drive",
    )
    parts = [along(part, ahead) for ahead, part in enumerate(parts)]

    fresh_same, fresh_away, own_same, own_away, far_same, far_away = call(
        functools.partial(readout_kernel, pairs, slices),
        [((2, 2 * tiles, NODES), f32)] * 2 + [((CORE, 2 * tiles, LANES), bf16)] * 4,
        (place, *parts, recur, *readout_weights),
        name="readout",
    )
    pattern = [(i, ((i + sections // 2) % sections) ^ 1) for i in range(sections)]
    far_same = along(far_same, pairs // 2)
    far_away = lax.ppermute(far_away, "col", pattern)
    own_away = across(own_away)
    fresh_away = across(fresh_away)
    return call(
        final_kernel,
        [((2, height, width), f32), ((block_rows, 2 * tiles, NODES), f32)],
        (place, own_same, own_away, far_same, far_away, gained_same, gained_away, fresh_same, fresh_away),
        [pltpu.VMEM((CORE * 2 * tiles, LANES), f32)],
        name="final",
    )


def solution(mesh):
    placed = (
        P(None, "row", "col"),
        P("row", "col", None),
        P("col", None),
        P(),
        P(),
        P(None, "col"),
        P(),
    )
    return jax.shard_map(
        local,
        mesh=mesh,
        in_specs=placed,
        out_specs=(P(None, "row", "col"), P("row", "col", None)),
        check_vma=False,
    )
```

```python
import functools

import jax
import jax.numpy as jnp
from jax import lax
from jax.experimental import pallas as pl
from jax.experimental.pallas import tpu as pltpu
from jax.sharding import PartitionSpec as P

CORE = 64
MARGIN = 4
NODES = 512
PATCH = 72
LANES = 128
STAGES = 4
GROUP = 8
REACH = MARGIN + STAGES
WINDOW = CORE + 2 * REACH

dispersion = 2.0
nonlinear = -0.7
time_step = 0.1

bf16 = jnp.bfloat16
f32 = jnp.float32
VMEM = pl.BlockSpec(memory_space=pltpu.VMEM)
SMEM = pl.BlockSpec(memory_space=pltpu.SMEM)


def call(kernel, outs, operands, scratch=(), megabytes=4, micros=1.0, name=None):
    return pl.pallas_call(
        kernel,
        out_shape=tuple(jax.ShapeDtypeStruct(*out) for out in outs),
        in_specs=[SMEM] + [VMEM] * (len(operands) - 1),
        out_specs=tuple(VMEM for _ in outs),
        scratch_shapes=list(scratch),
        compiler_params=pltpu.CompilerParams(vmem_limit_bytes=megabytes * 2**20),
        cost_estimate=pl.CostEstimate(flops=0, bytes_accessed=int(micros * 3.69e6), transcendentals=0),
        name=name,
    )(*operands)


def tendency(real_part, imag_part):
    def spread(values):
        rows, cols = values.shape
        return (
            pltpu.roll(values, 1, 0)
            + pltpu.roll(values, rows - 1, 0)
            + pltpu.roll(values, 1, 1)
            + pltpu.roll(values, cols - 1, 1)
            - 4.0 * values
        )

    real_spread = spread(real_part)
    imag_spread = spread(imag_part)
    modulus = real_part * real_part + imag_part * imag_part
    first = (
        real_part
        + real_spread
        - dispersion * imag_spread
        - modulus * (real_part - nonlinear * imag_part)
    )
    second = (
        imag_part
        + imag_spread
        + dispersion * real_spread
        - modulus * (imag_part + nonlinear * real_part)
    )
    return first, second


def forecast(start):
    slope = tendency(*start)
    total = slope
    for ahead, weight in ((0.5, 2.0), (0.5, 2.0), (1.0, 1.0)):
        at = tuple(s + ahead * time_step * k for s, k in zip(start, slope))
        slope = tendency(*at)
        total = tuple(t + weight * k for t, k in zip(total, slope))
    return tuple(s + time_step / 6.0 * t for s, t in zip(start, total))


def aligned(value):
    return pl.multiple_of(value, GROUP)


def both_cores(half, own, other):
    low = jnp.where(half == 0, own, other)
    high = jnp.where(half == 0, other, own)
    return low, high


def tile_of(values, tile):
    return values[:, tile * LANES : (tile + 1) * LANES]


def edges_kernel(place_ref, field_ref, out_ref):
    height, width = field_ref.shape[1:]
    lane = lax.broadcasted_iota(jnp.int32, (GROUP, LANES), 1)
    for channel in range(2):
        packed = None
        for group in range(height // GROUP):
            rows = slice(group * GROUP, (group + 1) * GROUP)
            left = pltpu.roll(field_ref[channel, rows, :LANES], group * STAGES, 1)
            right = pltpu.roll(field_ref[channel, rows, width - LANES :], (group + 1) * STAGES % LANES, 1)
            values = jnp.where(place_ref[0] == 0, left, right)
            packed = values if packed is None else jnp.where(lane >= group * STAGES, values, packed)
        out_ref[channel] = packed


def ends_kernel(place_ref, field_ref, other_ref, outer_ref, outer_other_ref, side_ref, out_ref):
    half = place_ref[0]
    height, width = field_ref.shape[1:]
    lane = lax.broadcasted_iota(jnp.int32, (GROUP, LANES), 1)
    at = aligned((height - REACH) * half)
    for channel in range(2):
        left, right = both_cores(half, outer_ref[channel], outer_other_ref[channel])
        for group in range(height // GROUP):
            after = pltpu.roll(right, (LANES - group * STAGES) % LANES, 1)
            before = pltpu.roll(left, (LANES - (group + 1) * STAGES) % LANES, 1)
            side_ref[channel, group * GROUP : (group + 1) * GROUP, :] = jnp.where(lane < LANES // 2, after, before)
        low, high = both_cores(half, field_ref[channel, pl.ds(at, REACH), :], other_ref[channel, pl.ds(at, REACH), :])
        out_ref[channel, :, :width] = low
        out_ref[channel, :, width : 2 * width] = high
        out_ref[channel, :, 2 * width :] = side_ref[channel, pl.ds(at, REACH), :]


def model_kernel(outer, place_ref, field_ref, other_ref, side_ref, *refs):
    if outer:
        ends_ref, inner_ref, *message_refs, model_ref, lines_ref, window_ref = refs
    else:
        lines_ref, model_ref = refs
    half = place_ref[0]
    height, width = field_ref.shape[1:]
    tiles = 2 * width // LANES
    length = WINDOW - REACH if outer else WINDOW
    at = aligned((height - length) * half) if outer else aligned(height // 2 - CORE - REACH + CORE * half)
    start = []
    for channel in range(2):
        own = field_ref[channel, pl.ds(at, length), :]
        other = other_ref[channel, pl.ds(at, length), :]
        cells = jnp.concatenate(both_cores(half, own, other) + (side_ref[channel, pl.ds(at, length), :],), 1)
        if outer:
            window_ref[channel, pl.ds(aligned(REACH * (1 - half)), length), :] = cells
            window_ref[channel, pl.ds(aligned(length * half), REACH), :] = ends_ref[channel]
            cells = window_ref[channel]
        start.append(cells)
    model = forecast(start)
    depth = lines_ref.shape[2]
    for channel, values in enumerate(tuple(start) + model):
        for tile in range(tiles):
            for part in range(PATCH // depth):
                at = MARGIN + part * depth
                lines_ref[channel * (PATCH // depth) + part, tile] = tile_of(values, tile)[at : at + depth].astype(bf16)
    for channel in range(2):
        model_ref[channel] = model[channel][REACH : REACH + CORE, : 2 * width]
    if outer:
        pairs = len(message_refs)
        for ahead, message_ref in enumerate(message_refs):
            of = lax.rem(place_ref[1] + ahead, pairs)
            message_ref[0] = inner_ref[of]
            message_ref[1] = lines_ref[of]


def gain_kernel(place_ref, inner_ref, outer_ref, gain_ref, same_ref, away_ref):
    half = place_ref[0]
    width = same_ref.shape[3]
    for channel in range(2):
        gain = gain_ref[channel]
        for row, model_ref in enumerate((inner_ref, outer_ref)):
            for tile in range(width // LANES):
                lanes = slice(tile * LANES, (tile + 1) * LANES)
                low = model_ref[channel, :, lanes]
                high = model_ref[channel, :, width + tile * LANES : width + (tile + 1) * LANES]
                same_ref[channel, row, :, lanes] = gain * jnp.where(half == 0, low, high)
                away_ref[channel, row, :, lanes] = gain * jnp.where(half == 0, high, low)


def drive_kernel(pairs, place_ref, *refs):
    patch_refs, weight_refs = refs[:pairs], refs[pairs : pairs + 2]
    out_refs, (cells_ref, left_ref) = refs[pairs + 2 : -2], refs[-2:]
    _, tiles, depth, _ = patch_refs[0].shape
    total = pairs * tiles
    for row in range(2):
        for pair in range(pairs):
            for tile in range(tiles):
                at = (row * total + pair * tiles + tile) * depth
                cells_ref[at : at + depth, :] = patch_refs[pair][row, tile].astype(f32)
    lane = lax.broadcasted_iota(jnp.int32, (total, LANES), 1)
    half = place_ref[0]
    lines = depth // 2
    width = lines * PATCH
    sums = None
    for which in range(2):
        begin = lines * (half if which == 0 else 1 - half)
        for row in range(2):
            held = [None, None]
            for line in range(lines):
                own = cells_ref[pl.ds(row * total * depth + begin + line, total, stride=depth), :]
                before = pltpu.roll(own, 1, 0)
                after = pltpu.roll(own, total - 1, 0)
                even = jnp.where(lane >= LANES - MARGIN, before, own)
                odd = jnp.where(lane < MARGIN, after, own)
                first = line * PATCH
                offset = first % LANES
                lanes = slice(first - offset, first - offset + LANES)
                for parity, (values, shift) in enumerate(((even, MARGIN), (odd, MARGIN + CORE))):
                    at = (row * 2 + parity) * total
                    moved = pltpu.roll(values, (first + shift) % LANES, 1)
                    current = moved if offset == 0 else jnp.where(lane >= offset, moved, held[parity])
                    if offset + PATCH >= LANES or line == lines - 1:
                        left_ref[which, at : at + total, lanes] = current.astype(bf16)
                        if line == lines - 1 and offset + PATCH > LANES:
                            more = slice(lanes.stop, lanes.stop + LANES)
                            left_ref[which, at : at + total, more] = moved.astype(bf16)
                        current = moved
                    held[parity] = current
        term = jnp.dot(left_ref[which, :, :width], weight_refs[which][...], preferred_element_type=f32)
        sums = term if sums is None else sums + term
    for pair, out_ref in enumerate(out_refs):
        pieces = []
        for of in (pair, (pair + pairs // 2) % pairs):
            for part in range(4):
                at = part * total + of * tiles
                pieces.append(sums[at : at + tiles])
        out_ref[...] = jnp.concatenate(pieces, 0).astype(bf16)


def part_kernel(place_ref, weight_ref, out_ref, done):
    rows = out_ref.shape[0]
    begin = pl.multiple_of(place_ref[4] * rows, rows)
    copy = pltpu.make_async_copy(weight_ref.at[pl.ds(begin, rows), :], out_ref, done)
    copy.start()
    copy.wait()


def row_part(place, weight):
    rows, columns = weight.shape
    return pl.pallas_call(
        part_kernel,
        out_shape=jax.ShapeDtypeStruct((rows // 2, columns), weight.dtype),
        in_specs=[SMEM, pl.BlockSpec(memory_space=pl.ANY)],
        out_specs=VMEM,
        scratch_shapes=[pltpu.SemaphoreType.DMA(())],
        compiler_params=pltpu.CompilerParams(vmem_limit_bytes=4 * 2**20),
        cost_estimate=pl.CostEstimate(flops=0, bytes_accessed=2_000_000, transcendentals=0),
        name="part",
    )(place, weight)


def previous_kernel(place_ref, states_ref, same_ref, away_ref):
    half = place_ref[0]
    block_rows, block_cols = states_ref.shape[:2]
    for away, out_ref in enumerate((same_ref, away_ref)):
        of = half if away == 0 else 1 - half
        pieces = []
        for row in (block_rows // 2 - 1 + of, (block_rows - 1) * of):
            values = states_ref[row]
            for parity in range(2):
                pieces += [values[column : column + 1] for column in range(parity, block_cols, 2)]
        out_ref[...] = jnp.concatenate(pieces, 0)


def recur_kernel(place_ref, same_ref, away_ref, weight_ref, bias_ref, out_ref):
    low, high = both_cores(place_ref[0], same_ref[...], away_ref[...])
    tiles = low.shape[0] // 4
    pieces = []
    for index in range(4):
        pieces += [values[index * tiles : (index + 1) * tiles] for values in (low, high)]
    previous = jnp.concatenate(pieces, 0).astype(bf16)
    out_ref[...] = jnp.dot(previous, weight_ref[...], preferred_element_type=f32) + bias_ref[...]


def halves(half, first, second):
    rows = first.shape[0]
    row = lax.broadcasted_iota(jnp.int32, first.shape, 0)
    low = jnp.where(row < rows // 2, first, pltpu.roll(second, rows // 2, 0))
    high = jnp.where(row < rows // 2, pltpu.roll(first, rows // 2, 0), second)
    return jnp.where(half == 0, low, high), jnp.where(half == 0, high, low)


def readout_kernel(pairs, slices, place_ref, *refs):
    parts, recur_refs, weights = refs[:pairs], refs[pairs : pairs + 2], refs[pairs + 2 : -6]
    fresh_same, fresh_away, own_same, own_away, far_same, far_away = refs[-6:]
    half = place_ref[0]
    total = jnp.concatenate([recur_ref[...] for recur_ref in recur_refs], 0)
    for part in parts:
        total = total + part[...].astype(f32)
    fresh = jnp.tanh(total)
    tiles = fresh.shape[0] // 8
    for row in range(2):
        at = row * 2 * tiles
        same, away = halves(half, fresh[at : at + tiles], fresh[at + tiles : at + 2 * tiles])
        fresh_same[row] = same
        fresh_away[row] = away
    readin = fresh.astype(bf16)
    lane = lax.broadcasted_iota(jnp.int32, (tiles, LANES), 1)
    swapped = place_ref[4] == 1
    low, high = readin[:, : NODES // 2], readin[:, NODES // 2 :]
    ordered = (jnp.where(swapped, high, low), jnp.where(swapped, low, high))
    for index in range(slices):
        if index < 2:
            products = jnp.dot(readin, weights[index][...], preferred_element_type=f32)
        else:
            products = sum(
                jnp.dot(ordered[part], weights[2 * index - 2 + part][...], preferred_element_type=f32)
                for part in range(2)
            )
        lines = products.shape[1] // CORE
        begin = lax.bitwise_xor(place_ref[2], index) * lines
        for tile in range(products.shape[1] // LANES):
            values = tile_of(products, tile)
            for of, (same_ref, away_ref) in enumerate(((own_same, own_away), (far_same, far_away))):
                pair = []
                for row in range(2):
                    at = (of * 2 + row) * 2 * tiles
                    low, high = values[at : at + tiles], values[at + tiles : at + 2 * tiles]
                    pair.append(
                        (
                            jnp.where(lane < CORE, low, pltpu.roll(high, CORE, 1)),
                            jnp.where(lane < CORE, pltpu.roll(low, CORE, 1), high),
                        )
                    )
                for line in range(2):
                    same, away = halves(half, pair[0][line], pair[1][line])
                    same_ref[begin + 2 * tile + line] = same.astype(bf16)
                    away_ref[begin + 2 * tile + line] = away.astype(bf16)


def final_kernel(
    place_ref,
    own_same,
    own_away,
    far_same,
    far_away,
    gained_same,
    gained_away,
    fresh_same,
    fresh_away,
    out_ref,
    states_ref,
    cells_ref,
):
    half = place_ref[0]
    side = place_ref[3]
    tiles = out_ref.shape[2] // LANES
    block_rows = out_ref.shape[1] // CORE
    rows = 2 * tiles
    for away, (own, far, gained, fresh) in enumerate(
        ((own_same, far_same, gained_same, fresh_same), (own_away, far_away, gained_away, fresh_away))
    ):
        of = half if away == 0 else 1 - half
        places = (block_rows // 2 - 1 + of, (block_rows - 1) * of)
        for opposite, values in enumerate((own, far)):
            channel = side if opposite == 0 else 1 - side
            cells_ref[...] = values[...].astype(f32).reshape(CORE * rows, LANES)
            for row in range(2):
                for tile in range(tiles):
                    lanes = slice(tile * LANES, (tile + 1) * LANES)
                    placed = cells_ref[pl.ds(row * tiles + tile, CORE, stride=rows), :]
                    at = pl.multiple_of(places[row] * CORE, CORE)
                    out_ref[channel, pl.ds(at, CORE), lanes] = gained[channel, row, :, lanes] + placed
        for row in range(2):
            for column in range(2 * tiles):
                at = (column % 2) * tiles + column // 2
                states_ref[places[row], column : column + 1, :] = fresh[row, at : at + 1, :]


def after(values, *others):
    return lax.optimization_barrier((values,) + others)[0]


def local(field, states, input_weight, recurrent_weight, bias, output_weight, model_gain):
    height, width = field.shape[1:]
    sections = lax.axis_size("col")
    bands = lax.axis_size("row")
    pairs = sections // 2
    block_rows = height // CORE
    tiles = width // LANES
    depth = 4 * PATCH // pairs
    slices = sections // 2
    column = lax.axis_index("col")
    band = lax.axis_index("row")
    half = column % 2
    place = jnp.stack([half, column // 2, column % slices, column // slices, band % 2])

    def across(values):
        return lax.ppermute(values, "col", [(i, i ^ 1) for i in range(sections)])

    def along(values, ahead):
        if ahead % pairs == 0:
            return values
        return lax.ppermute(values, "col", [(i, (i + 2 * ahead) % sections) for i in range(sections)])

    other = across(field)
    (edges,) = call(edges_kernel, [((2, GROUP, LANES), f32)], (place, field), name="edges")
    pattern = [(i, (i + (1 if i % 2 else -1)) % sections) for i in range(sections)]
    edges = lax.ppermute(edges, "col", pattern)
    edges_other = across(after(edges, other))
    side, ends = call(
        ends_kernel,
        [((2, height, LANES), f32), ((2, REACH, 2 * width + LANES), f32)],
        (place, field, other, edges, edges_other),
        name="ends",
    )
    pattern = []
    for item in range(bands):
        for core in range(0, sections, 2):
            pattern.append((item * sections + core, (item - 1) % bands * sections + core + 1))
            pattern.append((item * sections + core + 1, (item + 1) % bands * sections + core))
    ends = lax.ppermute(ends, ("row", "col"), pattern)

    weight_other = across(after(input_weight, edges_other))
    readout_weights = [output_weight, across(after(output_weight, edges_other))]
    part = row_part(place, after(output_weight, edges))
    firsts = [lax.ppermute(part, "col", [(i, i ^ index) for i in range(sections)]) for index in range(2, slices, 2)]

    lines = ((pairs, 2 * tiles, depth, LANES), bf16)
    model = ((2, CORE, 2 * width), f32)
    inner_lines, inner_model = call(
        functools.partial(model_kernel, False),
        [lines, model],
        (place, field, other, side),
        megabytes=8,
        micros=3.3,
        name="inner_model",
    )
    *messages, outer_model = call(
        functools.partial(model_kernel, True),
        [((2, *lines[0][1:]), bf16)] * pairs + [model],
        (place, field, other, side, after(ends, inner_model, weight_other, readout_weights[1]), inner_lines),
        [pltpu.VMEM(*lines), pltpu.VMEM((2, WINDOW, 2 * width + LANES), f32)],
        12,
        3.3,
        name="outer_model",
    )
    messages = lax.optimization_barrier((*messages, *firsts))
    messages, firsts = messages[:pairs], messages[pairs:]
    patches = [along(messages[-ahead % pairs], -ahead) for ahead in range(pairs)]
    gain = jnp.concatenate([model_gain, model_gain], 2)
    gained_same, gained_away = call(
        gain_kernel,
        [((2, 2, CORE, width), f32)] * 2,
        (place, inner_model, outer_model, gain),
        micros=1.0,
        name="gain",
    )
    gained_away = across(gained_away)

    previous = call(
        previous_kernel,
        [((block_rows * tiles, NODES), f32)] * 2,
        (place, after(states, outer_model)),
        micros=0.5,
        name="previous",
    )
    (recur,) = call(
        recur_kernel,
        [((2 * block_rows * tiles, NODES), f32)],
        (place, previous[0], across(after(previous[1], gained_away)), recurrent_weight, bias[None]),
        micros=0.5,
        name="recur",
    )

    recurs = (recur, along(recur, pairs // 2))
    total = pairs * 2 * tiles
    weight_own = after(input_weight, gained_away, *recurs)
    parts = call(
        functools.partial(drive_kernel, pairs),
        [((8 * 2 * tiles, NODES), bf16)] * pairs,
        (place, *patches, weight_own, weight_other),
        [
            pltpu.VMEM((2 * total * depth, LANES), f32),
            pltpu.VMEM((2, 4 * total, -(-depth // 2 * PATCH // LANES) * LANES), bf16),
        ],
        10,
        4.0,
        name="drive",
    )
    for first in firsts:
        second = lax.ppermute(first, "row", [(i, i ^ 1) for i in range(bands)])
        readout_weights += [first, second, across(after(first, parts[0])), across(after(second, parts[0]))]
    parts = [along(part, ahead) for ahead, part in enumerate(parts)]

    fresh_same, fresh_away, own_same, own_away, far_same, far_away = call(
        functools.partial(readout_kernel, pairs, slices),
        [((2, 2 * tiles, NODES), f32)] * 2 + [((CORE, 2 * tiles, LANES), bf16)] * 4,
        (place, *parts, *recurs, *readout_weights),
        megabytes=12,
        micros=2.5,
        name="readout",
    )
    pattern = [(i, ((i + sections // 2) % sections) ^ 1) for i in range(sections)]
    far_same = along(far_same, pairs // 2)
    far_away = lax.ppermute(far_away, "col", pattern)
    own_away = across(own_away)
    fresh_away = across(fresh_away)
    return call(
        final_kernel,
        [((2, height, width), f32), ((block_rows, 2 * tiles, NODES), f32)],
        (place, own_same, own_away, far_same, far_away, gained_same, gained_away, fresh_same, fresh_away),
        [pltpu.VMEM((CORE * 2 * tiles, LANES), f32)],
        4,
        2.0,
        name="final",
    )


def solution(mesh):
    placed = (
        P(None, "row", "col"),
        P("row", "col", None),
        P("col", None),
        P(),
        P(),
        P(None, "col"),
        P(),
    )
    return jax.shard_map(
        local,
        mesh=mesh,
        in_specs=placed,
        out_specs=(P(None, "row", "col"), P("row", "col", None)),
        check_vma=False,
    )
```

```python
import functools

import jax
import jax.numpy as jnp
from jax import lax
from jax.experimental import pallas as pl
from jax.experimental.pallas import tpu as pltpu
from jax.sharding import PartitionSpec as P

CORE = 64
MARGIN = 4
NODES = 512
PATCH = 72
LANES = 128
STAGES = 4
GROUP = 8
REACH = MARGIN + STAGES
WINDOW = CORE + 2 * REACH

dispersion = 2.0
nonlinear = -0.7
time_step = 0.1

bf16 = jnp.bfloat16
f32 = jnp.float32
VMEM = pl.BlockSpec(memory_space=pltpu.VMEM)
SMEM = pl.BlockSpec(memory_space=pltpu.SMEM)


def call(kernel, outs, operands, scratch=(), megabytes=4, micros=1.0, name=None):
    return pl.pallas_call(
        kernel,
        out_shape=tuple(jax.ShapeDtypeStruct(*out) for out in outs),
        in_specs=[SMEM] + [VMEM] * (len(operands) - 1),
        out_specs=tuple(VMEM for _ in outs),
        scratch_shapes=list(scratch),
        compiler_params=pltpu.CompilerParams(vmem_limit_bytes=megabytes * 2**20),
        cost_estimate=pl.CostEstimate(flops=0, bytes_accessed=int(micros * 3.69e6), transcendentals=0),
        name=name,
    )(*operands)


def tendency(real_part, imag_part):
    def spread(values):
        rows, cols = values.shape
        return (
            pltpu.roll(values, 1, 0)
            + pltpu.roll(values, rows - 1, 0)
            + pltpu.roll(values, 1, 1)
            + pltpu.roll(values, cols - 1, 1)
            - 4.0 * values
        )

    real_spread = spread(real_part)
    imag_spread = spread(imag_part)
    modulus = real_part * real_part + imag_part * imag_part
    first = (
        real_part
        + real_spread
        - dispersion * imag_spread
        - modulus * (real_part - nonlinear * imag_part)
    )
    second = (
        imag_part
        + imag_spread
        + dispersion * real_spread
        - modulus * (imag_part + nonlinear * real_part)
    )
    return first, second


def forecast(start):
    slope = tendency(*start)
    total = slope
    for ahead, weight in ((0.5, 2.0), (0.5, 2.0), (1.0, 1.0)):
        at = tuple(s + ahead * time_step * k for s, k in zip(start, slope))
        slope = tendency(*at)
        total = tuple(t + weight * k for t, k in zip(total, slope))
    return tuple(s + time_step / 6.0 * t for s, t in zip(start, total))


def aligned(value):
    return pl.multiple_of(value, GROUP)


def both_cores(half, own, other):
    low = jnp.where(half == 0, own, other)
    high = jnp.where(half == 0, other, own)
    return low, high


def tile_of(values, tile):
    return values[:, tile * LANES : (tile + 1) * LANES]


def edges_kernel(place_ref, field_ref, out_ref):
    height, width = field_ref.shape[1:]
    lane = lax.broadcasted_iota(jnp.int32, (GROUP, LANES), 1)
    for channel in range(2):
        packed = None
        for group in range(height // GROUP):
            rows = slice(group * GROUP, (group + 1) * GROUP)
            left = pltpu.roll(field_ref[channel, rows, :LANES], group * STAGES, 1)
            right = pltpu.roll(field_ref[channel, rows, width - LANES :], (group + 1) * STAGES % LANES, 1)
            values = jnp.where(place_ref[0] == 0, left, right)
            packed = values if packed is None else jnp.where(lane >= group * STAGES, values, packed)
        out_ref[channel] = packed


def ends_kernel(place_ref, field_ref, other_ref, outer_ref, outer_other_ref, side_ref, out_ref):
    half = place_ref[0]
    height, width = field_ref.shape[1:]
    lane = lax.broadcasted_iota(jnp.int32, (GROUP, LANES), 1)
    at = aligned((height - REACH) * half)
    for channel in range(2):
        left, right = both_cores(half, outer_ref[channel], outer_other_ref[channel])
        for group in range(height // GROUP):
            after = pltpu.roll(right, (LANES - group * STAGES) % LANES, 1)
            before = pltpu.roll(left, (LANES - (group + 1) * STAGES) % LANES, 1)
            side_ref[channel, group * GROUP : (group + 1) * GROUP, :] = jnp.where(lane < LANES // 2, after, before)
        low, high = both_cores(half, field_ref[channel, pl.ds(at, REACH), :], other_ref[channel, pl.ds(at, REACH), :])
        out_ref[channel, :, :width] = low
        out_ref[channel, :, width : 2 * width] = high
        out_ref[channel, :, 2 * width :] = side_ref[channel, pl.ds(at, REACH), :]


def model_kernel(outer, place_ref, field_ref, other_ref, side_ref, *refs):
    if outer:
        ends_ref, inner_ref, *message_refs, model_ref, lines_ref, window_ref = refs
    else:
        lines_ref, model_ref = refs
    half = place_ref[0]
    height, width = field_ref.shape[1:]
    tiles = 2 * width // LANES
    length = WINDOW - REACH if outer else WINDOW
    at = aligned((height - length) * half) if outer else aligned(height // 2 - CORE - REACH + CORE * half)
    start = []
    for channel in range(2):
        own = field_ref[channel, pl.ds(at, length), :]
        other = other_ref[channel, pl.ds(at, length), :]
        cells = jnp.concatenate(both_cores(half, own, other) + (side_ref[channel, pl.ds(at, length), :],), 1)
        if outer:
            window_ref[channel, pl.ds(aligned(REACH * (1 - half)), length), :] = cells
            window_ref[channel, pl.ds(aligned(length * half), REACH), :] = ends_ref[channel]
            cells = window_ref[channel]
        start.append(cells)
    model = forecast(start)
    depth = lines_ref.shape[2]
    for channel, values in enumerate(tuple(start) + model):
        for tile in range(tiles):
            for part in range(PATCH // depth):
                at = MARGIN + part * depth
                lines_ref[channel * (PATCH // depth) + part, tile] = tile_of(values, tile)[at : at + depth].astype(bf16)
    for channel in range(2):
        model_ref[channel] = model[channel][REACH : REACH + CORE, : 2 * width]
    if outer:
        pairs = len(message_refs)
        for ahead, message_ref in enumerate(message_refs):
            of = lax.rem(place_ref[1] + ahead, pairs)
            message_ref[0] = inner_ref[of]
            message_ref[1] = lines_ref[of]


def gain_kernel(place_ref, inner_ref, outer_ref, gain_ref, *refs):
    count = len(refs) // 2 - 1
    first_refs, (same_ref, away_ref), quarter_refs = refs[:count], refs[count : count + 2], refs[count + 2 :]
    for first_ref, quarter_ref in zip(first_refs, quarter_refs):
        rows = quarter_ref.shape[0]
        begin = pl.multiple_of(place_ref[4] * (first_ref.shape[0] - rows), rows)
        quarter_ref[...] = first_ref[pl.ds(begin, rows), :]
    half = place_ref[0]
    width = same_ref.shape[3]
    for channel in range(2):
        gain = gain_ref[channel]
        for row, model_ref in enumerate((inner_ref, outer_ref)):
            for tile in range(width // LANES):
                lanes = slice(tile * LANES, (tile + 1) * LANES)
                low = model_ref[channel, :, lanes]
                high = model_ref[channel, :, width + tile * LANES : width + (tile + 1) * LANES]
                same_ref[channel, row, :, lanes] = gain * jnp.where(half == 0, low, high)
                away_ref[channel, row, :, lanes] = gain * jnp.where(half == 0, high, low)


def drive_kernel(pairs, place_ref, *refs):
    patch_refs, weight_refs = refs[:pairs], refs[pairs : pairs + 2]
    out_refs, (cells_ref, left_ref) = refs[pairs + 2 : -2], refs[-2:]
    _, tiles, depth, _ = patch_refs[0].shape
    total = pairs * tiles
    for row in range(2):
        for pair in range(pairs):
            for tile in range(tiles):
                at = (row * total + pair * tiles + tile) * depth
                cells_ref[at : at + depth, :] = patch_refs[pair][row, tile].astype(f32)
    lane = lax.broadcasted_iota(jnp.int32, (total, LANES), 1)
    half = place_ref[0]
    lines = depth // 2
    width = lines * PATCH
    sums = None
    for which in range(2):
        begin = lines * (half if which == 0 else 1 - half)
        for row in range(2):
            held = [None, None]
            for line in range(lines):
                own = cells_ref[pl.ds(row * total * depth + begin + line, total, stride=depth), :]
                before = pltpu.roll(own, 1, 0)
                after = pltpu.roll(own, total - 1, 0)
                even = jnp.where(lane >= LANES - MARGIN, before, own)
                odd = jnp.where(lane < MARGIN, after, own)
                first = line * PATCH
                offset = first % LANES
                lanes = slice(first - offset, first - offset + LANES)
                for parity, (values, shift) in enumerate(((even, MARGIN), (odd, MARGIN + CORE))):
                    at = (row * 2 + parity) * total
                    moved = pltpu.roll(values, (first + shift) % LANES, 1)
                    current = moved if offset == 0 else jnp.where(lane >= offset, moved, held[parity])
                    if offset + PATCH >= LANES or line == lines - 1:
                        left_ref[which, at : at + total, lanes] = current.astype(bf16)
                        if line == lines - 1 and offset + PATCH > LANES:
                            more = slice(lanes.stop, lanes.stop + LANES)
                            left_ref[which, at : at + total, more] = moved.astype(bf16)
                        current = moved
                    held[parity] = current
        term = jnp.dot(left_ref[which, :, :width], weight_refs[which][...], preferred_element_type=f32)
        sums = term if sums is None else sums + term
    for pair, out_ref in enumerate(out_refs):
        pieces = []
        for of in (pair, (pair + pairs // 2) % pairs):
            for part in range(4):
                at = part * total + of * tiles
                pieces.append(sums[at : at + tiles])
        out_ref[...] = jnp.concatenate(pieces, 0).astype(bf16)


def part_kernel(place_ref, weight_ref, out_ref, done):
    rows = out_ref.shape[0]
    begin = pl.multiple_of(place_ref[4] * (weight_ref.shape[0] - rows), LANES)
    copy = pltpu.make_async_copy(weight_ref.at[pl.ds(begin, rows), :], out_ref, done)
    copy.start()
    copy.wait()


def row_part(place, weight):
    rows, columns = weight.shape
    return pl.pallas_call(
        part_kernel,
        out_shape=jax.ShapeDtypeStruct((rows - rows // 4, columns), weight.dtype),
        in_specs=[SMEM, pl.BlockSpec(memory_space=pltpu.HBM)],
        out_specs=VMEM,
        scratch_shapes=[pltpu.SemaphoreType.DMA(())],
        compiler_params=pltpu.CompilerParams(vmem_limit_bytes=4 * 2**20),
        cost_estimate=pl.CostEstimate(flops=0, bytes_accessed=2_000_000, transcendentals=0),
        name="part",
    )(place, weight)


def previous_kernel(place_ref, states_ref, same_ref, away_ref):
    half = place_ref[0]
    block_rows, block_cols = states_ref.shape[:2]
    for away, out_ref in enumerate((same_ref, away_ref)):
        of = half if away == 0 else 1 - half
        pieces = []
        for row in (block_rows // 2 - 1 + of, (block_rows - 1) * of):
            values = states_ref[row]
            for parity in range(2):
                pieces += [values[column : column + 1] for column in range(parity, block_cols, 2)]
        out_ref[...] = jnp.concatenate(pieces, 0)


def recur_kernel(place_ref, same_ref, away_ref, weight_ref, bias_ref, out_ref):
    low, high = both_cores(place_ref[0], same_ref[...], away_ref[...])
    tiles = low.shape[0] // 4
    pieces = []
    for index in range(4):
        pieces += [values[index * tiles : (index + 1) * tiles] for values in (low, high)]
    previous = jnp.concatenate(pieces, 0).astype(bf16)
    out_ref[...] = jnp.dot(previous, weight_ref[...], preferred_element_type=f32) + bias_ref[...]


def halves(half, first, second):
    rows = first.shape[0]
    row = lax.broadcasted_iota(jnp.int32, first.shape, 0)
    low = jnp.where(row < rows // 2, first, pltpu.roll(second, rows // 2, 0))
    high = jnp.where(row < rows // 2, pltpu.roll(first, rows // 2, 0), second)
    return jnp.where(half == 0, low, high), jnp.where(half == 0, high, low)


def readout_kernel(pairs, place_ref, *refs):
    parts, recur_refs, weights = refs[:pairs], refs[pairs : pairs + 2], refs[pairs + 2 : -6]
    fresh_same, fresh_away, own_same, own_away, far_same, far_away = refs[-6:]
    half = place_ref[0]
    total = jnp.concatenate([recur_ref[...] for recur_ref in recur_refs], 0)
    for part in parts:
        total = total + part[...].astype(f32)
    fresh = jnp.tanh(total)
    tiles = fresh.shape[0] // 8
    for row in range(2):
        at = row * 2 * tiles
        same, away = halves(half, fresh[at : at + tiles], fresh[at + tiles : at + 2 * tiles])
        fresh_same[row] = same
        fresh_away[row] = away
    readin = fresh.astype(bf16)
    lane = lax.broadcasted_iota(jnp.int32, (tiles, LANES), 1)
    odd = place_ref[4] == 1
    quarter = NODES // 4
    most = jnp.where(odd, readin[:, quarter:], readin[:, : NODES - quarter])
    rest = jnp.where(odd, readin[:, :quarter], readin[:, NODES - quarter :])
    for index in range(len(weights) // 2 + 1):
        if index < 2:
            products = jnp.dot(readin, weights[index][...], preferred_element_type=f32)
        else:
            head, tail = weights[2 * index - 2 : 2 * index]
            products = jnp.dot(most, head[...], preferred_element_type=f32)
            products = products + jnp.dot(rest, tail[...], preferred_element_type=f32)
        lines = products.shape[1] // CORE
        begin = lax.bitwise_xor(place_ref[2], index) * lines
        for tile in range(products.shape[1] // LANES):
            values = tile_of(products, tile)
            for of, (same_ref, away_ref) in enumerate(((own_same, own_away), (far_same, far_away))):
                pair = []
                for row in range(2):
                    at = (of * 2 + row) * 2 * tiles
                    low, high = values[at : at + tiles], values[at + tiles : at + 2 * tiles]
                    pair.append(
                        (
                            jnp.where(lane < CORE, low, pltpu.roll(high, CORE, 1)),
                            jnp.where(lane < CORE, pltpu.roll(low, CORE, 1), high),
                        )
                    )
                for line in range(2):
                    same, away = halves(half, pair[0][line], pair[1][line])
                    same_ref[begin + 2 * tile + line] = same.astype(bf16)
                    away_ref[begin + 2 * tile + line] = away.astype(bf16)


def final_kernel(
    place_ref,
    own_same,
    own_away,
    far_same,
    far_away,
    gained_same,
    gained_away,
    fresh_same,
    fresh_away,
    out_ref,
    states_ref,
    cells_ref,
):
    half = place_ref[0]
    side = place_ref[3]
    tiles = out_ref.shape[2] // LANES
    block_rows = out_ref.shape[1] // CORE
    rows = 2 * tiles
    for away, (own, far, gained, fresh) in enumerate(
        ((own_same, far_same, gained_same, fresh_same), (own_away, far_away, gained_away, fresh_away))
    ):
        of = half if away == 0 else 1 - half
        places = (block_rows // 2 - 1 + of, (block_rows - 1) * of)
        for opposite, values in enumerate((own, far)):
            channel = side if opposite == 0 else 1 - side
            cells_ref[...] = values[...].astype(f32).reshape(CORE * rows, LANES)
            for row in range(2):
                for tile in range(tiles):
                    lanes = slice(tile * LANES, (tile + 1) * LANES)
                    placed = cells_ref[pl.ds(row * tiles + tile, CORE, stride=rows), :]
                    at = pl.multiple_of(places[row] * CORE, CORE)
                    out_ref[channel, pl.ds(at, CORE), lanes] = gained[channel, row, :, lanes] + placed
        for row in range(2):
            for column in range(2 * tiles):
                at = (column % 2) * tiles + column // 2
                states_ref[places[row], column : column + 1, :] = fresh[row, at : at + 1, :]


def after(values, *others):
    return lax.optimization_barrier((values,) + others)[0]


def local(field, states, input_weight, recurrent_weight, bias, output_weight, model_gain):
    height, width = field.shape[1:]
    sections = lax.axis_size("col")
    bands = lax.axis_size("row")
    pairs = sections // 2
    block_rows = height // CORE
    tiles = width // LANES
    depth = 4 * PATCH // pairs
    slices = sections // 2
    column = lax.axis_index("col")
    band = lax.axis_index("row")
    half = column % 2
    place = jnp.stack([half, column // 2, column % slices, column // slices, band % 2])

    def across(values):
        return lax.ppermute(values, "col", [(i, i ^ 1) for i in range(sections)])

    def along(values, ahead):
        if ahead % pairs == 0:
            return values
        return lax.ppermute(values, "col", [(i, (i + 2 * ahead) % sections) for i in range(sections)])

    other = across(field)
    (edges,) = call(edges_kernel, [((2, GROUP, LANES), f32)], (place, field), name="edges")
    pattern = [(i, (i + (1 if i % 2 else -1)) % sections) for i in range(sections)]
    edges = lax.ppermute(edges, "col", pattern)
    edges_other = across(after(edges, other))
    side, ends = call(
        ends_kernel,
        [((2, height, LANES), f32), ((2, REACH, 2 * width + LANES), f32)],
        (place, field, other, edges, edges_other),
        name="ends",
    )
    pattern = []
    for item in range(bands):
        for core in range(0, sections, 2):
            pattern.append((item * sections + core, (item - 1) % bands * sections + core + 1))
            pattern.append((item * sections + core + 1, (item + 1) % bands * sections + core))
    ends = lax.ppermute(ends, ("row", "col"), pattern)

    weight_other = across(after(input_weight, edges_other))
    readout_weights = [output_weight, across(after(output_weight, edges_other))]
    part = row_part(place, after(output_weight, side))
    patterns = [[(i, i ^ index) for i in range(sections)] for index in range(2, slices, 2)]
    firsts = [lax.ppermute(part, "col", pattern) for pattern in patterns]

    lines = ((pairs, 2 * tiles, depth, LANES), bf16)
    model = ((2, CORE, 2 * width), f32)
    inner_lines, inner_model = call(
        functools.partial(model_kernel, False),
        [lines, model],
        (place, field, other, side),
        megabytes=8,
        micros=3.3,
        name="inner_model",
    )
    *messages, outer_model = call(
        functools.partial(model_kernel, True),
        [((2, *lines[0][1:]), bf16)] * pairs + [model],
        (place, field, other, side, after(ends, inner_model, weight_other, readout_weights[1]), inner_lines),
        [pltpu.VMEM(*lines), pltpu.VMEM((2, WINDOW, 2 * width + LANES), f32)],
        12,
        3.3,
        name="outer_model",
    )
    patches = [along(messages[-ahead % pairs], -ahead) for ahead in range(pairs)]
    previous = call(
        previous_kernel,
        [((block_rows * tiles, NODES), f32)] * 2,
        (place, after(states, outer_model)),
        micros=0.5,
        name="previous",
    )
    (recur,) = call(
        recur_kernel,
        [((2 * block_rows * tiles, NODES), f32)],
        (place, previous[0], across(previous[1]), recurrent_weight, bias[None]),
        micros=0.5,
        name="recur",
    )

    gain = jnp.concatenate([model_gain, model_gain], 2)
    gained_same, gained_away, *quarters = call(
        gain_kernel,
        [((2, 2, CORE, width), f32)] * 2 + [((NODES // 4, first.shape[1]), bf16) for first in firsts],
        (place, inner_model, after(outer_model, recur), gain, *firsts),
        micros=1.0,
        name="gain",
    )
    recurs = (recur, along(recur, pairs // 2))
    total = pairs * 2 * tiles
    seconds = [lax.ppermute(quarter, "row", [(i, i ^ 1) for i in range(bands)]) for quarter in quarters]
    weight_own = after(input_weight, gained_same, *recurs, *seconds)
    parts = call(
        functools.partial(drive_kernel, pairs),
        [((8 * 2 * tiles, NODES), bf16)] * pairs,
        (place, *patches, weight_own, weight_other),
        [
            pltpu.VMEM((2 * total * depth, LANES), f32),
            pltpu.VMEM((2, 4 * total, -(-depth // 2 * PATCH // LANES) * LANES), bf16),
        ],
        10,
        4.0,
        name="drive",
    )
    parts = [along(part, ahead) for ahead, part in enumerate(parts)]
    for first, second in zip(firsts, seconds):
        readout_weights += [first, second, across(after(first, parts[0])), across(after(second, parts[0]))]

    fresh_same, fresh_away, own_same, own_away, far_same, far_away = call(
        functools.partial(readout_kernel, pairs),
        [((2, 2 * tiles, NODES), f32)] * 2 + [((CORE, 2 * tiles, LANES), bf16)] * 4,
        (place, *parts, *recurs, *readout_weights),
        megabytes=12,
        micros=2.5,
        name="readout",
    )
    pattern = [(i, ((i + sections // 2) % sections) ^ 1) for i in range(sections)]
    far_same = along(far_same, pairs // 2)
    far_away = lax.ppermute(far_away, "col", pattern)
    own_away = across(own_away)
    fresh_away = across(fresh_away)
    gained_away = across(after(gained_away, own_same))
    return call(
        final_kernel,
        [((2, height, width), f32), ((block_rows, 2 * tiles, NODES), f32)],
        (place, own_same, own_away, far_same, far_away, gained_same, gained_away, fresh_same, fresh_away),
        [pltpu.VMEM((CORE * 2 * tiles, LANES), f32)],
        4,
        2.0,
        name="final",
    )


def solution(mesh):
    placed = (
        P(None, "row", "col"),
        P("row", "col", None),
        P("col", None),
        P(),
        P(),
        P(None, "col"),
        P(),
    )
    return jax.shard_map(
        local,
        mesh=mesh,
        in_specs=placed,
        out_specs=(P(None, "row", "col"), P("row", "col", None)),
        check_vma=False,
    )
```

```python
import functools

import jax
import jax.numpy as jnp
from jax import lax
from jax.experimental import pallas as pl
from jax.experimental.pallas import tpu as pltpu
from jax.sharding import PartitionSpec as P

CORE = 64
MARGIN = 4
NODES = 512
PATCH = 72
LANES = 128
STAGES = 4
GROUP = 8
REACH = MARGIN + STAGES
WINDOW = CORE + 2 * REACH

dispersion = 2.0
nonlinear = -0.7
time_step = 0.1

bf16 = jnp.bfloat16
f32 = jnp.float32
VMEM = pl.BlockSpec(memory_space=pltpu.VMEM)
SMEM = pl.BlockSpec(memory_space=pltpu.SMEM)


def call(kernel, outs, operands, scratch=(), megabytes=4, micros=1.0, name=None):
    return pl.pallas_call(
        kernel,
        out_shape=tuple(jax.ShapeDtypeStruct(*out) for out in outs),
        in_specs=[SMEM] + [VMEM] * (len(operands) - 1),
        out_specs=tuple(VMEM for _ in outs),
        scratch_shapes=list(scratch),
        compiler_params=pltpu.CompilerParams(vmem_limit_bytes=megabytes * 2**20),
        cost_estimate=pl.CostEstimate(flops=0, bytes_accessed=int(micros * 3.69e6), transcendentals=0),
        name=name,
    )(*operands)


def tendency(real_part, imag_part):
    def spread(values):
        rows, cols = values.shape
        return (
            pltpu.roll(values, 1, 0)
            + pltpu.roll(values, rows - 1, 0)
            + pltpu.roll(values, 1, 1)
            + pltpu.roll(values, cols - 1, 1)
            - 4.0 * values
        )

    real_spread = spread(real_part)
    imag_spread = spread(imag_part)
    modulus = real_part * real_part + imag_part * imag_part
    first = (
        real_part
        + real_spread
        - dispersion * imag_spread
        - modulus * (real_part - nonlinear * imag_part)
    )
    second = (
        imag_part
        + imag_spread
        + dispersion * real_spread
        - modulus * (imag_part + nonlinear * real_part)
    )
    return first, second


def forecast(start):
    slope = tendency(*start)
    total = slope
    for ahead, weight in ((0.5, 2.0), (0.5, 2.0), (1.0, 1.0)):
        at = tuple(s + ahead * time_step * k for s, k in zip(start, slope))
        slope = tendency(*at)
        total = tuple(t + weight * k for t, k in zip(total, slope))
    return tuple(s + time_step / 6.0 * t for s, t in zip(start, total))


def aligned(value):
    return pl.multiple_of(value, GROUP)


def both_cores(half, own, other):
    low = jnp.where(half == 0, own, other)
    high = jnp.where(half == 0, other, own)
    return low, high


def tile_of(values, tile):
    return values[:, tile * LANES : (tile + 1) * LANES]


def edges_kernel(place_ref, field_ref, out_ref):
    height, width = field_ref.shape[1:]
    lane = lax.broadcasted_iota(jnp.int32, (GROUP, LANES), 1)
    for channel in range(2):
        packed = None
        for group in range(height // GROUP):
            rows = slice(group * GROUP, (group + 1) * GROUP)
            left = pltpu.roll(field_ref[channel, rows, :LANES], group * STAGES, 1)
            right = pltpu.roll(field_ref[channel, rows, width - LANES :], (group + 1) * STAGES % LANES, 1)
            values = jnp.where(place_ref[0] == 0, left, right)
            packed = values if packed is None else jnp.where(lane >= group * STAGES, values, packed)
        out_ref[channel] = packed


def ends_kernel(place_ref, field_ref, other_ref, outer_ref, outer_other_ref, side_ref, out_ref):
    half = place_ref[0]
    height, width = field_ref.shape[1:]
    lane = lax.broadcasted_iota(jnp.int32, (GROUP, LANES), 1)
    at = aligned((height - REACH) * half)
    for channel in range(2):
        left, right = both_cores(half, outer_ref[channel], outer_other_ref[channel])
        for group in range(height // GROUP):
            after = pltpu.roll(right, (LANES - group * STAGES) % LANES, 1)
            before = pltpu.roll(left, (LANES - (group + 1) * STAGES) % LANES, 1)
            side_ref[channel, group * GROUP : (group + 1) * GROUP, :] = jnp.where(lane < LANES // 2, after, before)
        low, high = both_cores(half, field_ref[channel, pl.ds(at, REACH), :], other_ref[channel, pl.ds(at, REACH), :])
        out_ref[channel, :, :width] = low
        out_ref[channel, :, width : 2 * width] = high
        out_ref[channel, :, 2 * width :] = side_ref[channel, pl.ds(at, REACH), :]


def upper_first(half, row):
    return half if row else 1 - half


def model_kernel(outer, place_ref, field_ref, other_ref, side_ref, *refs):
    if outer:
        ends_ref, inner_ref, *message_refs, model_ref, lines_ref, window_ref = refs
    else:
        lines_ref, model_ref = refs
    half = place_ref[0]
    height, width = field_ref.shape[1:]
    tiles = 2 * width // LANES
    length = WINDOW - REACH if outer else WINDOW
    at = aligned((height - length) * half) if outer else aligned(height // 2 - CORE - REACH + CORE * half)
    start = []
    for channel in range(2):
        own = field_ref[channel, pl.ds(at, length), :]
        other = other_ref[channel, pl.ds(at, length), :]
        cells = jnp.concatenate(both_cores(half, own, other) + (side_ref[channel, pl.ds(at, length), :],), 1)
        if outer:
            window_ref[channel, pl.ds(aligned(REACH * (1 - half)), length), :] = cells
            window_ref[channel, pl.ds(aligned(length * half), REACH), :] = ends_ref[channel]
            cells = window_ref[channel]
        start.append(cells)
    model = forecast(start)
    depth = lines_ref.shape[2]
    for channel, values in enumerate(tuple(start) + model):
        for tile in range(tiles):
            for part in range(PATCH // depth):
                at = MARGIN + part * depth
                lines_ref[channel * (PATCH // depth) + part, tile] = tile_of(values, tile)[at : at + depth].astype(bf16)
    for channel in range(2):
        model_ref[channel] = model[channel][REACH : REACH + CORE, : 2 * width]
    if outer:
        pairs = len(message_refs)
        for ahead, message_ref in enumerate(message_refs):
            of = lax.rem(place_ref[1] + ahead, pairs)
            for row, source_ref in enumerate((inner_ref, lines_ref)):
                if message_ref.shape[0] == 1:
                    at = pl.multiple_of(CORE * upper_first(half, row), CORE)
                    message_ref[0, :, pl.ds(at, PATCH), :] = source_ref[of]
                else:
                    message_ref[row] = source_ref[of]


def gain_kernel(place_ref, inner_ref, outer_ref, gain_ref, *refs):
    count = len(refs) // 2 - 1
    first_refs, (same_ref, away_ref), quarter_refs = refs[:count], refs[count : count + 2], refs[count + 2 :]
    for first_ref, quarter_ref in zip(first_refs, quarter_refs):
        rows = quarter_ref.shape[0]
        begin = pl.multiple_of(place_ref[4] * (first_ref.shape[0] - rows), rows)
        quarter_ref[...] = first_ref[pl.ds(begin, rows), :]
    half = place_ref[0]
    width = same_ref.shape[3]
    for channel in range(2):
        gain = gain_ref[channel]
        for row, model_ref in enumerate((inner_ref, outer_ref)):
            for tile in range(width // LANES):
                lanes = slice(tile * LANES, (tile + 1) * LANES)
                low = model_ref[channel, :, lanes]
                high = model_ref[channel, :, width + tile * LANES : width + (tile + 1) * LANES]
                same_ref[channel, row, :, lanes] = gain * jnp.where(half == 0, low, high)
                away_ref[channel, row, :, lanes] = gain * jnp.where(half == 0, high, low)


def drive_kernel(pairs, place_ref, *refs):
    patch_refs, weight_refs = refs[:pairs], refs[pairs : pairs + 2]
    out_refs, (cells_ref, left_ref) = refs[pairs + 2 : -2], refs[-2:]
    kinds, tiles, stride, _ = patch_refs[0].shape
    depth = PATCH if kinds == 1 else stride
    total = pairs * tiles
    for row in range(kinds):
        for pair in range(pairs):
            for tile in range(tiles):
                at = (row * total + pair * tiles + tile) * stride
                cells_ref[at : at + stride, :] = patch_refs[pair][row, tile].astype(f32)
    lane = lax.broadcasted_iota(jnp.int32, (total, LANES), 1)
    half = place_ref[0]
    lines = depth // 2
    width = lines * PATCH
    sums = None
    for which in range(2):
        begin = lines * (half if which == 0 else 1 - half)
        for row in range(2):
            held = [None, None]
            for line in range(lines):
                at = CORE * upper_first(half, row) if kinds == 1 else row * total * depth
                own = cells_ref[pl.ds(at + begin + line, total, stride=stride), :]
                before = pltpu.roll(own, 1, 0)
                after = pltpu.roll(own, total - 1, 0)
                even = jnp.where(lane >= LANES - MARGIN, before, own)
                odd = jnp.where(lane < MARGIN, after, own)
                first = line * PATCH
                offset = first % LANES
                lanes = slice(first - offset, first - offset + LANES)
                for parity, (values, shift) in enumerate(((even, MARGIN), (odd, MARGIN + CORE))):
                    at = (row * 2 + parity) * total
                    moved = pltpu.roll(values, (first + shift) % LANES, 1)
                    current = moved if offset == 0 else jnp.where(lane >= offset, moved, held[parity])
                    if offset + PATCH >= LANES or line == lines - 1:
                        left_ref[which, at : at + total, lanes] = current.astype(bf16)
                        if line == lines - 1 and offset + PATCH > LANES:
                            more = slice(lanes.stop, lanes.stop + LANES)
                            left_ref[which, at : at + total, more] = moved.astype(bf16)
                        current = moved
                    held[parity] = current
        term = jnp.dot(left_ref[which, :, :width], weight_refs[which][...], preferred_element_type=f32)
        sums = term if sums is None else sums + term
    for pair, out_ref in enumerate(out_refs):
        pieces = []
        for of in (pair, (pair + pairs // 2) % pairs):
            for part in range(4):
                at = part * total + of * tiles
                pieces.append(sums[at : at + tiles])
        out_ref[...] = jnp.concatenate(pieces, 0).astype(bf16)


def part_kernel(place_ref, weight_ref, out_ref, done):
    rows = out_ref.shape[0]
    begin = pl.multiple_of(place_ref[4] * (weight_ref.shape[0] - rows), LANES)
    copy = pltpu.make_async_copy(weight_ref.at[pl.ds(begin, rows), :], out_ref, done)
    copy.start()
    copy.wait()


def row_part(place, weight):
    rows, columns = weight.shape
    return pl.pallas_call(
        part_kernel,
        out_shape=jax.ShapeDtypeStruct((rows - rows // 4, columns), weight.dtype),
        in_specs=[SMEM, pl.BlockSpec(memory_space=pltpu.HBM)],
        out_specs=VMEM,
        scratch_shapes=[pltpu.SemaphoreType.DMA(())],
        compiler_params=pltpu.CompilerParams(vmem_limit_bytes=4 * 2**20),
        cost_estimate=pl.CostEstimate(flops=0, bytes_accessed=2_000_000, transcendentals=0),
        name="part",
    )(place, weight)


def previous_kernel(place_ref, states_ref, same_ref, away_ref):
    half = place_ref[0]
    block_rows, block_cols = states_ref.shape[:2]
    for away, out_ref in enumerate((same_ref, away_ref)):
        of = half if away == 0 else 1 - half
        pieces = []
        for row in (block_rows // 2 - 1 + of, (block_rows - 1) * of):
            values = states_ref[row]
            for parity in range(2):
                pieces += [values[column : column + 1] for column in range(parity, block_cols, 2)]
        out_ref[...] = jnp.concatenate(pieces, 0)


def recur_kernel(place_ref, same_ref, away_ref, weight_ref, bias_ref, out_ref):
    low, high = both_cores(place_ref[0], same_ref[...], away_ref[...])
    tiles = low.shape[0] // 4
    pieces = []
    for index in range(4):
        pieces += [values[index * tiles : (index + 1) * tiles] for values in (low, high)]
    previous = jnp.concatenate(pieces, 0).astype(bf16)
    out_ref[...] = jnp.dot(previous, weight_ref[...], preferred_element_type=f32) + bias_ref[...]


def halves(half, first, second):
    rows = first.shape[0]
    row = lax.broadcasted_iota(jnp.int32, first.shape, 0)
    low = jnp.where(row < rows // 2, first, pltpu.roll(second, rows // 2, 0))
    high = jnp.where(row < rows // 2, pltpu.roll(first, rows // 2, 0), second)
    return jnp.where(half == 0, low, high), jnp.where(half == 0, high, low)


def readout_kernel(pairs, place_ref, *refs):
    parts, recur_refs, weights = refs[:pairs], refs[pairs : pairs + 2], refs[pairs + 2 : -6]
    fresh_same, fresh_away, own_same, own_away, far_same, far_away = refs[-6:]
    half = place_ref[0]
    total = jnp.concatenate([recur_ref[...] for recur_ref in recur_refs], 0)
    for part in parts:
        total = total + part[...].astype(f32)
    fresh = jnp.tanh(total)
    tiles = fresh.shape[0] // 8
    for row in range(2):
        at = row * 2 * tiles
        same, away = halves(half, fresh[at : at + tiles], fresh[at + tiles : at + 2 * tiles])
        fresh_same[row] = same
        fresh_away[row] = away
    readin = fresh.astype(bf16)
    lane = lax.broadcasted_iota(jnp.int32, (tiles, LANES), 1)
    odd = place_ref[4] == 1
    quarter = NODES // 4
    most = jnp.where(odd, readin[:, quarter:], readin[:, : NODES - quarter])
    rest = jnp.where(odd, readin[:, :quarter], readin[:, NODES - quarter :])
    for index in range(len(weights) // 2 + 1):
        if index < 2:
            products = jnp.dot(readin, weights[index][...], preferred_element_type=f32)
        else:
            head, tail = weights[2 * index - 2 : 2 * index]
            products = jnp.dot(most, head[...], preferred_element_type=f32)
            products = products + jnp.dot(rest, tail[...], preferred_element_type=f32)
        lines = products.shape[1] // CORE
        begin = lax.bitwise_xor(place_ref[2], index) * lines
        for tile in range(products.shape[1] // LANES):
            values = tile_of(products, tile)
            for of, (same_ref, away_ref) in enumerate(((own_same, own_away), (far_same, far_away))):
                pair = []
                for row in range(2):
                    at = (of * 2 + row) * 2 * tiles
                    low, high = values[at : at + tiles], values[at + tiles : at + 2 * tiles]
                    pair.append(
                        (
                            jnp.where(lane < CORE, low, pltpu.roll(high, CORE, 1)),
                            jnp.where(lane < CORE, pltpu.roll(low, CORE, 1), high),
                        )
                    )
                for line in range(2):
                    same, away = halves(half, pair[0][line], pair[1][line])
                    same_ref[begin + 2 * tile + line] = same.astype(bf16)
                    away_ref[begin + 2 * tile + line] = away.astype(bf16)


def final_kernel(
    place_ref,
    own_same,
    own_away,
    far_same,
    far_away,
    gained_same,
    gained_away,
    fresh_same,
    fresh_away,
    out_ref,
    states_ref,
    cells_ref,
):
    half = place_ref[0]
    side = place_ref[3]
    tiles = out_ref.shape[2] // LANES
    block_rows = out_ref.shape[1] // CORE
    rows = 2 * tiles
    for away, (own, far, gained, fresh) in enumerate(
        ((own_same, far_same, gained_same, fresh_same), (own_away, far_away, gained_away, fresh_away))
    ):
        of = half if away == 0 else 1 - half
        places = (block_rows // 2 - 1 + of, (block_rows - 1) * of)
        for opposite, values in enumerate((own, far)):
            channel = side if opposite == 0 else 1 - side
            cells_ref[...] = values[...].astype(f32).reshape(CORE * rows, LANES)
            for row in range(2):
                for tile in range(tiles):
                    lanes = slice(tile * LANES, (tile + 1) * LANES)
                    placed = cells_ref[pl.ds(row * tiles + tile, CORE, stride=rows), :]
                    at = pl.multiple_of(places[row] * CORE, CORE)
                    out_ref[channel, pl.ds(at, CORE), lanes] = gained[channel, row, :, lanes] + placed
        for row in range(2):
            for column in range(2 * tiles):
                at = (column % 2) * tiles + column // 2
                states_ref[places[row], column : column + 1, :] = fresh[row, at : at + 1, :]


def after(values, *others):
    return lax.optimization_barrier((values,) + others)[0]


def local(field, states, input_weight, recurrent_weight, bias, output_weight, model_gain):
    height, width = field.shape[1:]
    sections = lax.axis_size("col")
    bands = lax.axis_size("row")
    pairs = sections // 2
    block_rows = height // CORE
    tiles = width // LANES
    depth = 4 * PATCH // pairs
    slices = sections // 2
    column = lax.axis_index("col")
    band = lax.axis_index("row")
    half = column % 2
    place = jnp.stack([half, column // 2, column % slices, column // slices, band % 2])

    def across(values):
        return lax.ppermute(values, "col", [(i, i ^ 1) for i in range(sections)])

    def along(values, ahead):
        if ahead % pairs == 0:
            return values
        return lax.ppermute(values, "col", [(i, (i + 2 * ahead) % sections) for i in range(sections)])

    other = across(field)
    (edges,) = call(edges_kernel, [((2, GROUP, LANES), f32)], (place, field), name="edges")
    pattern = [(i, (i + (1 if i % 2 else -1)) % sections) for i in range(sections)]
    edges = lax.ppermute(edges, "col", pattern)
    edges_other = across(after(edges, other))
    side, ends = call(
        ends_kernel,
        [((2, height, LANES), f32), ((2, REACH, 2 * width + LANES), f32)],
        (place, field, other, edges, edges_other),
        name="ends",
    )
    pattern = []
    for item in range(bands):
        for core in range(0, sections, 2):
            pattern.append((item * sections + core, (item - 1) % bands * sections + core + 1))
            pattern.append((item * sections + core + 1, (item + 1) % bands * sections + core))
    ends = lax.ppermute(ends, ("row", "col"), pattern)

    weight_other = across(after(input_weight, edges_other))
    readout_weights = [output_weight, across(after(output_weight, edges_other))]
    part = row_part(place, after(output_weight, side))
    patterns = [[(i, i ^ index) for i in range(sections)] for index in range(2, slices, 2)]
    firsts = [lax.ppermute(part, "col", pattern) for pattern in patterns]

    lines = ((pairs, 2 * tiles, depth, LANES), bf16)
    model = ((2, CORE, 2 * width), f32)
    message = (1, 2 * tiles, PATCH + CORE, LANES) if depth == PATCH else (2, 2 * tiles, depth, LANES)
    inner_lines, inner_model = call(
        functools.partial(model_kernel, False),
        [lines, model],
        (place, field, other, side),
        megabytes=8,
        micros=3.3,
        name="inner_model",
    )
    *messages, outer_model = call(
        functools.partial(model_kernel, True),
        [(message, bf16)] * pairs + [model],
        (place, field, other, side, after(ends, inner_model, weight_other, readout_weights[1]), inner_lines),
        [pltpu.VMEM(*lines), pltpu.VMEM((2, WINDOW, 2 * width + LANES), f32)],
        12,
        3.3,
        name="outer_model",
    )
    patches = [along(messages[-ahead % pairs], -ahead) for ahead in range(pairs)]
    previous = call(
        previous_kernel,
        [((block_rows * tiles, NODES), f32)] * 2,
        (place, after(states, outer_model)),
        micros=0.5,
        name="previous",
    )
    (recur,) = call(
        recur_kernel,
        [((2 * block_rows * tiles, NODES), f32)],
        (place, previous[0], across(previous[1]), recurrent_weight, bias[None]),
        micros=0.5,
        name="recur",
    )

    gain = jnp.concatenate([model_gain, model_gain], 2)
    gained_same, gained_away, *quarters = call(
        gain_kernel,
        [((2, 2, CORE, width), f32)] * 2 + [((NODES // 4, first.shape[1]), bf16) for first in firsts],
        (place, inner_model, after(outer_model, recur), gain, *firsts),
        micros=1.0,
        name="gain",
    )
    recurs = (recur, along(recur, pairs // 2))
    total = pairs * 2 * tiles
    seconds = [lax.ppermute(quarter, "row", [(i, i ^ 1) for i in range(bands)]) for quarter in quarters]
    weight_own = after(input_weight, gained_same, *recurs, *seconds)
    parts = call(
        functools.partial(drive_kernel, pairs),
        [((8 * 2 * tiles, NODES), bf16)] * pairs,
        (place, *patches, weight_own, weight_other),
        [
            pltpu.VMEM((message[0] * total * message[2], LANES), f32),
            pltpu.VMEM((2, 4 * total, -(-depth // 2 * PATCH // LANES) * LANES), bf16),
        ],
        10,
        4.0,
        name="drive",
    )
    parts = [along(part, ahead) for ahead, part in enumerate(parts)]
    for first, second in zip(firsts, seconds):
        readout_weights += [first, second, across(after(first, parts[0])), across(after(second, parts[0]))]

    fresh_same, fresh_away, own_same, own_away, far_same, far_away = call(
        functools.partial(readout_kernel, pairs),
        [((2, 2 * tiles, NODES), f32)] * 2 + [((CORE, 2 * tiles, LANES), bf16)] * 4,
        (place, *parts, *recurs, *readout_weights),
        megabytes=12,
        micros=2.5,
        name="readout",
    )
    pattern = [(i, ((i + sections // 2) % sections) ^ 1) for i in range(sections)]
    far_same = along(far_same, pairs // 2)
    far_away = lax.ppermute(far_away, "col", pattern)
    own_away = across(own_away)
    fresh_away = across(fresh_away)
    gained_away = across(after(gained_away, own_same))
    return call(
        final_kernel,
        [((2, height, width), f32), ((block_rows, 2 * tiles, NODES), f32)],
        (place, own_same, own_away, far_same, far_away, gained_same, gained_away, fresh_same, fresh_away),
        [pltpu.VMEM((CORE * 2 * tiles, LANES), f32)],
        4,
        2.0,
        name="final",
    )


def solution(mesh):
    placed = (
        P(None, "row", "col"),
        P("row", "col", None),
        P("col", None),
        P(),
        P(),
        P(None, "col"),
        P(),
    )
    return jax.shard_map(
        local,
        mesh=mesh,
        in_specs=placed,
        out_specs=(P(None, "row", "col"), P("row", "col", None)),
        check_vma=False,
    )
```

```python
import functools

import jax
import jax.numpy as jnp
from jax import lax
from jax.experimental import pallas as pl
from jax.experimental.pallas import tpu as pltpu
from jax.sharding import PartitionSpec as P

CORE = 64
MARGIN = 4
NODES = 512
PATCH = 72
LANES = 128
STAGES = 4
GROUP = 8
REACH = MARGIN + STAGES
WINDOW = CORE + 2 * REACH

dispersion = 2.0
nonlinear = -0.7
time_step = 0.1

bf16 = jnp.bfloat16
f32 = jnp.float32
VMEM = pl.BlockSpec(memory_space=pltpu.VMEM)
SMEM = pl.BlockSpec(memory_space=pltpu.SMEM)


def call(kernel, outs, operands, scratch=(), megabytes=4, micros=1.0, name=None):
    return pl.pallas_call(
        kernel,
        out_shape=tuple(jax.ShapeDtypeStruct(*out) for out in outs),
        in_specs=[SMEM] + [VMEM] * (len(operands) - 1),
        out_specs=tuple(VMEM for _ in outs),
        scratch_shapes=list(scratch),
        compiler_params=pltpu.CompilerParams(vmem_limit_bytes=megabytes * 2**20),
        cost_estimate=pl.CostEstimate(flops=0, bytes_accessed=int(micros * 3.69e6), transcendentals=0),
        name=name,
    )(*operands)


def tendency(real_part, imag_part):
    def spread(values):
        rows, cols = values.shape
        return (
            pltpu.roll(values, 1, 0)
            + pltpu.roll(values, rows - 1, 0)
            + pltpu.roll(values, 1, 1)
            + pltpu.roll(values, cols - 1, 1)
            - 4.0 * values
        )

    real_spread = spread(real_part)
    imag_spread = spread(imag_part)
    modulus = real_part * real_part + imag_part * imag_part
    first = (
        real_part
        + real_spread
        - dispersion * imag_spread
        - modulus * (real_part - nonlinear * imag_part)
    )
    second = (
        imag_part
        + imag_spread
        + dispersion * real_spread
        - modulus * (imag_part + nonlinear * real_part)
    )
    return first, second


def forecast(start):
    slope = tendency(*start)
    total = slope
    for ahead, weight in ((0.5, 2.0), (0.5, 2.0), (1.0, 1.0)):
        at = tuple(s + ahead * time_step * k for s, k in zip(start, slope))
        slope = tendency(*at)
        total = tuple(t + weight * k for t, k in zip(total, slope))
    return tuple(s + time_step / 6.0 * t for s, t in zip(start, total))


def aligned(value):
    return pl.multiple_of(value, GROUP)


def both_cores(half, own, other):
    low = jnp.where(half == 0, own, other)
    high = jnp.where(half == 0, other, own)
    return low, high


def tile_of(values, tile):
    return values[:, tile * LANES : (tile + 1) * LANES]


def edges_kernel(place_ref, field_ref, out_ref):
    height, width = field_ref.shape[1:]
    lane = lax.broadcasted_iota(jnp.int32, (GROUP, LANES), 1)
    for channel in range(2):
        packed = None
        for group in range(height // GROUP):
            rows = slice(group * GROUP, (group + 1) * GROUP)
            left = pltpu.roll(field_ref[channel, rows, :LANES], group * STAGES, 1)
            right = pltpu.roll(field_ref[channel, rows, width - LANES :], (group + 1) * STAGES % LANES, 1)
            values = jnp.where(place_ref[0] == 0, left, right)
            packed = values if packed is None else jnp.where(lane >= group * STAGES, values, packed)
        out_ref[channel] = packed


def ends_kernel(place_ref, field_ref, other_ref, outer_ref, outer_other_ref, side_ref, out_ref):
    half = place_ref[0]
    height, width = field_ref.shape[1:]
    lane = lax.broadcasted_iota(jnp.int32, (GROUP, LANES), 1)
    at = aligned((height - REACH) * half)
    for channel in range(2):
        left, right = both_cores(half, outer_ref[channel], outer_other_ref[channel])
        for group in range(height // GROUP):
            after = pltpu.roll(right, (LANES - group * STAGES) % LANES, 1)
            before = pltpu.roll(left, (LANES - (group + 1) * STAGES) % LANES, 1)
            side_ref[channel, group * GROUP : (group + 1) * GROUP, :] = jnp.where(lane < LANES // 2, after, before)
        low, high = both_cores(half, field_ref[channel, pl.ds(at, REACH), :], other_ref[channel, pl.ds(at, REACH), :])
        out_ref[channel, :, :width] = low
        out_ref[channel, :, width : 2 * width] = high
        out_ref[channel, :, 2 * width :] = side_ref[channel, pl.ds(at, REACH), :]


def upper_first(half, row):
    return half if row else 1 - half


def model_kernel(outer, place_ref, field_ref, other_ref, side_ref, *refs):
    if outer:
        ends_ref, inner_ref, *message_refs, model_ref, lines_ref, window_ref = refs
    else:
        lines_ref, model_ref = refs
    half = place_ref[0]
    height, width = field_ref.shape[1:]
    tiles = 2 * width // LANES
    length = WINDOW - REACH if outer else WINDOW
    at = aligned((height - length) * half) if outer else aligned(height // 2 - CORE - REACH + CORE * half)
    start = []
    for channel in range(2):
        own = field_ref[channel, pl.ds(at, length), :]
        other = other_ref[channel, pl.ds(at, length), :]
        cells = jnp.concatenate(both_cores(half, own, other) + (side_ref[channel, pl.ds(at, length), :],), 1)
        if outer:
            window_ref[channel, pl.ds(aligned(REACH * (1 - half)), length), :] = cells
            window_ref[channel, pl.ds(aligned(length * half), REACH), :] = ends_ref[channel]
            cells = window_ref[channel]
        start.append(cells)
    model = forecast(start)
    depth = lines_ref.shape[2]
    for channel, values in enumerate(tuple(start) + model):
        for tile in range(tiles):
            for part in range(PATCH // depth):
                at = MARGIN + part * depth
                lines_ref[channel * (PATCH // depth) + part, tile] = tile_of(values, tile)[at : at + depth].astype(bf16)
    for channel in range(2):
        model_ref[channel] = model[channel][REACH : REACH + CORE, : 2 * width]
    if outer:
        pairs = len(message_refs)
        for ahead, message_ref in enumerate(message_refs):
            of = lax.rem(place_ref[1] + ahead, pairs)
            for row, source_ref in enumerate((inner_ref, lines_ref)):
                if message_ref.shape[0] == 1:
                    at = pl.multiple_of(CORE * upper_first(half, row), CORE)
                    message_ref[0, :, pl.ds(at, PATCH), :] = source_ref[of]
                else:
                    message_ref[row] = source_ref[of]


def gain_kernel(place_ref, inner_ref, outer_ref, gain_ref, *refs):
    count = len(refs) // 2 - 1
    first_refs, (same_ref, away_ref), quarter_refs = refs[:count], refs[count : count + 2], refs[count + 2 :]
    for first_ref, quarter_ref in zip(first_refs, quarter_refs):
        rows = quarter_ref.shape[0]
        begin = pl.multiple_of(place_ref[4] * (first_ref.shape[0] - rows), rows)
        quarter_ref[...] = first_ref[pl.ds(begin, rows), :]
    half = place_ref[0]
    width = same_ref.shape[3]
    for channel in range(2):
        gain = gain_ref[channel]
        for row, model_ref in enumerate((inner_ref, outer_ref)):
            for tile in range(width // LANES):
                lanes = slice(tile * LANES, (tile + 1) * LANES)
                low = model_ref[channel, :, lanes]
                high = model_ref[channel, :, width + tile * LANES : width + (tile + 1) * LANES]
                same_ref[channel, row, :, lanes] = gain * jnp.where(half == 0, low, high)
                away_ref[channel, row, :, lanes] = gain * jnp.where(half == 0, high, low)


def drive_kernel(pairs, place_ref, *refs):
    patch_refs, weight_refs, recur_ref = refs[:pairs], refs[pairs : pairs + 2], refs[pairs + 2]
    out_refs, (cells_ref, left_ref) = refs[pairs + 3 : -2], refs[-2:]
    kinds, tiles, stride, _ = patch_refs[0].shape
    depth = PATCH if kinds == 1 else stride
    total = pairs * tiles
    for row in range(kinds):
        for pair in range(pairs):
            for tile in range(tiles):
                at = (row * total + pair * tiles + tile) * stride
                cells_ref[at : at + stride, :] = patch_refs[pair][row, tile].astype(f32)
    lane = lax.broadcasted_iota(jnp.int32, (total, LANES), 1)
    half = place_ref[0]
    lines = depth // 2
    width = lines * PATCH
    sums = None
    for which in range(2):
        begin = lines * (half if which == 0 else 1 - half)
        for row in range(2):
            held = [None, None]
            for line in range(lines):
                at = CORE * upper_first(half, row) if kinds == 1 else row * total * depth
                own = cells_ref[pl.ds(at + begin + line, total, stride=stride), :]
                before = pltpu.roll(own, 1, 0)
                after = pltpu.roll(own, total - 1, 0)
                even = jnp.where(lane >= LANES - MARGIN, before, own)
                odd = jnp.where(lane < MARGIN, after, own)
                first = line * PATCH
                offset = first % LANES
                lanes = slice(first - offset, first - offset + LANES)
                for parity, (values, shift) in enumerate(((even, MARGIN), (odd, MARGIN + CORE))):
                    at = (row * 2 + parity) * total
                    moved = pltpu.roll(values, (first + shift) % LANES, 1)
                    current = moved if offset == 0 else jnp.where(lane >= offset, moved, held[parity])
                    if offset + PATCH >= LANES or line == lines - 1:
                        left_ref[which, at : at + total, lanes] = current.astype(bf16)
                        if line == lines - 1 and offset + PATCH > LANES:
                            more = slice(lanes.stop, lanes.stop + LANES)
                            left_ref[which, at : at + total, more] = moved.astype(bf16)
                        current = moved
                    held[parity] = current
        term = jnp.dot(left_ref[which, :, :width], weight_refs[which][...], preferred_element_type=f32)
        sums = term if sums is None else sums + term
    for pair, out_ref in enumerate(out_refs):
        pieces = []
        for of in (pair, (pair + pairs // 2) % pairs):
            for part in range(4):
                at = part * total + of * tiles
                piece = sums[at : at + tiles]
                if of == 0:
                    piece = piece + recur_ref[part * tiles : (part + 1) * tiles, :]
                pieces.append(piece)
        out_ref[...] = jnp.concatenate(pieces, 0).astype(bf16)


def part_kernel(place_ref, weight_ref, out_ref, done):
    rows = out_ref.shape[0]
    begin = pl.multiple_of(place_ref[4] * (weight_ref.shape[0] - rows), LANES)
    copy = pltpu.make_async_copy(weight_ref.at[pl.ds(begin, rows), :], out_ref, done)
    copy.start()
    copy.wait()


def row_part(place, weight):
    rows, columns = weight.shape
    return pl.pallas_call(
        part_kernel,
        out_shape=jax.ShapeDtypeStruct((rows - rows // 4, columns), weight.dtype),
        in_specs=[SMEM, pl.BlockSpec(memory_space=pltpu.HBM)],
        out_specs=VMEM,
        scratch_shapes=[pltpu.SemaphoreType.DMA(())],
        compiler_params=pltpu.CompilerParams(vmem_limit_bytes=4 * 2**20),
        cost_estimate=pl.CostEstimate(flops=0, bytes_accessed=2_000_000, transcendentals=0),
        name="part",
    )(place, weight)


def previous_kernel(place_ref, states_ref, same_ref, away_ref):
    half = place_ref[0]
    block_rows, block_cols = states_ref.shape[:2]
    for away, out_ref in enumerate((same_ref, away_ref)):
        of = half if away == 0 else 1 - half
        pieces = []
        for row in (block_rows // 2 - 1 + of, (block_rows - 1) * of):
            values = states_ref[row]
            for parity in range(2):
                pieces += [values[column : column + 1] for column in range(parity, block_cols, 2)]
        out_ref[...] = jnp.concatenate(pieces, 0)


def recur_kernel(place_ref, same_ref, away_ref, weight_ref, bias_ref, out_ref):
    low, high = both_cores(place_ref[0], same_ref[...], away_ref[...])
    tiles = low.shape[0] // 4
    pieces = []
    for index in range(4):
        pieces += [values[index * tiles : (index + 1) * tiles] for values in (low, high)]
    previous = jnp.concatenate(pieces, 0).astype(bf16)
    out_ref[...] = jnp.dot(previous, weight_ref[...], preferred_element_type=f32) + bias_ref[...]


def halves(half, first, second):
    rows = first.shape[0]
    row = lax.broadcasted_iota(jnp.int32, first.shape, 0)
    low = jnp.where(row < rows // 2, first, pltpu.roll(second, rows // 2, 0))
    high = jnp.where(row < rows // 2, pltpu.roll(first, rows // 2, 0), second)
    return jnp.where(half == 0, low, high), jnp.where(half == 0, high, low)


def readout_kernel(pairs, place_ref, *refs):
    parts, weights = refs[:pairs], refs[pairs:-6]
    fresh_same, fresh_away, own_same, own_away, far_same, far_away = refs[-6:]
    half = place_ref[0]
    total = sum(part[...].astype(f32) for part in parts)
    fresh = jnp.tanh(total)
    tiles = fresh.shape[0] // 8
    for row in range(2):
        at = row * 2 * tiles
        same, away = halves(half, fresh[at : at + tiles], fresh[at + tiles : at + 2 * tiles])
        fresh_same[row] = same
        fresh_away[row] = away
    readin = fresh.astype(bf16)
    lane = lax.broadcasted_iota(jnp.int32, (tiles, LANES), 1)
    odd = place_ref[4] == 1
    quarter = NODES // 4
    most = jnp.where(odd, readin[:, quarter:], readin[:, : NODES - quarter])
    rest = jnp.where(odd, readin[:, :quarter], readin[:, NODES - quarter :])
    for index in range(len(weights) // 2 + 1):
        if index < 2:
            products = jnp.dot(readin, weights[index][...], preferred_element_type=f32)
        else:
            head, tail = weights[2 * index - 2 : 2 * index]
            products = jnp.dot(most, head[...], preferred_element_type=f32)
            products = products + jnp.dot(rest, tail[...], preferred_element_type=f32)
        lines = products.shape[1] // CORE
        begin = lax.bitwise_xor(place_ref[2], index) * lines
        for tile in range(products.shape[1] // LANES):
            values = tile_of(products, tile)
            for of, (same_ref, away_ref) in enumerate(((own_same, own_away), (far_same, far_away))):
                pair = []
                for row in range(2):
                    at = (of * 2 + row) * 2 * tiles
                    low, high = values[at : at + tiles], values[at + tiles : at + 2 * tiles]
                    pair.append(
                        (
                            jnp.where(lane < CORE, low, pltpu.roll(high, CORE, 1)),
                            jnp.where(lane < CORE, pltpu.roll(low, CORE, 1), high),
                        )
                    )
                for line in range(2):
                    same, away = halves(half, pair[0][line], pair[1][line])
                    same_ref[begin + 2 * tile + line] = same.astype(bf16)
                    away_ref[begin + 2 * tile + line] = away.astype(bf16)


def final_kernel(
    place_ref,
    own_same,
    own_away,
    far_same,
    far_away,
    gained_same,
    gained_away,
    fresh_same,
    fresh_away,
    out_ref,
    states_ref,
    cells_ref,
):
    half = place_ref[0]
    side = place_ref[3]
    tiles = out_ref.shape[2] // LANES
    block_rows = out_ref.shape[1] // CORE
    rows = 2 * tiles
    for away, (own, far, gained, fresh) in enumerate(
        ((own_same, far_same, gained_same, fresh_same), (own_away, far_away, gained_away, fresh_away))
    ):
        of = half if away == 0 else 1 - half
        places = (block_rows // 2 - 1 + of, (block_rows - 1) * of)
        for opposite, values in enumerate((own, far)):
            channel = side if opposite == 0 else 1 - side
            cells_ref[...] = values[...].astype(f32).reshape(CORE * rows, LANES)
            for row in range(2):
                for tile in range(tiles):
                    lanes = slice(tile * LANES, (tile + 1) * LANES)
                    placed = cells_ref[pl.ds(row * tiles + tile, CORE, stride=rows), :]
                    at = pl.multiple_of(places[row] * CORE, CORE)
                    out_ref[channel, pl.ds(at, CORE), lanes] = gained[channel, row, :, lanes] + placed
        for row in range(2):
            for column in range(2 * tiles):
                at = (column % 2) * tiles + column // 2
                states_ref[places[row], column : column + 1, :] = fresh[row, at : at + 1, :]


def after(values, *others):
    return lax.optimization_barrier((values,) + others)[0]


def local(field, states, input_weight, recurrent_weight, bias, output_weight, model_gain):
    height, width = field.shape[1:]
    sections = lax.axis_size("col")
    bands = lax.axis_size("row")
    pairs = sections // 2
    block_rows = height // CORE
    tiles = width // LANES
    depth = 4 * PATCH // pairs
    slices = sections // 2
    column = lax.axis_index("col")
    band = lax.axis_index("row")
    half = column % 2
    place = jnp.stack([half, column // 2, column % slices, column // slices, band % 2])

    def across(values):
        return lax.ppermute(values, "col", [(i, i ^ 1) for i in range(sections)])

    def along(values, ahead):
        if ahead % pairs == 0:
            return values
        return lax.ppermute(values, "col", [(i, (i + 2 * ahead) % sections) for i in range(sections)])

    other = across(field)
    (edges,) = call(edges_kernel, [((2, GROUP, LANES), f32)], (place, field), name="edges")
    pattern = [(i, (i + (1 if i % 2 else -1)) % sections) for i in range(sections)]
    edges = lax.ppermute(edges, "col", pattern)
    edges_other = across(after(edges, other))
    side, ends = call(
        ends_kernel,
        [((2, height, LANES), f32), ((2, REACH, 2 * width + LANES), f32)],
        (place, field, other, edges, edges_other),
        name="ends",
    )
    pattern = []
    for item in range(bands):
        for core in range(0, sections, 2):
            pattern.append((item * sections + core, (item - 1) % bands * sections + core + 1))
            pattern.append((item * sections + core + 1, (item + 1) % bands * sections + core))
    ends = lax.ppermute(ends, ("row", "col"), pattern)

    weight_other = across(after(input_weight, edges_other))
    readout_weights = [output_weight, across(after(output_weight, edges_other))]
    part = row_part(place, after(output_weight, side))
    patterns = [[(i, i ^ index) for i in range(sections)] for index in range(2, slices, 2)]
    firsts = [lax.ppermute(part, "col", pattern) for pattern in patterns]

    lines = ((pairs, 2 * tiles, depth, LANES), bf16)
    model = ((2, CORE, 2 * width), f32)
    message = (1, 2 * tiles, PATCH + CORE, LANES) if depth == PATCH else (2, 2 * tiles, depth, LANES)
    inner_lines, inner_model = call(
        functools.partial(model_kernel, False),
        [lines, model],
        (place, field, other, side),
        megabytes=8,
        micros=3.3,
        name="inner_model",
    )
    *messages, outer_model = call(
        functools.partial(model_kernel, True),
        [(message, bf16)] * pairs + [model],
        (place, field, other, side, after(ends, inner_model, weight_other, readout_weights[1]), inner_lines),
        [pltpu.VMEM(*lines), pltpu.VMEM((2, WINDOW, 2 * width + LANES), f32)],
        12,
        3.3,
        name="outer_model",
    )
    patches = [along(messages[-ahead % pairs], -ahead) for ahead in range(pairs)]
    previous = call(
        previous_kernel,
        [((block_rows * tiles, NODES), f32)] * 2,
        (place, after(states, outer_model)),
        micros=0.5,
        name="previous",
    )
    (recur,) = call(
        recur_kernel,
        [((2 * block_rows * tiles, NODES), f32)],
        (place, previous[0], across(previous[1]), recurrent_weight, bias[None]),
        micros=0.5,
        name="recur",
    )

    gain = jnp.concatenate([model_gain, model_gain], 2)
    gained_same, gained_away, *quarters = call(
        gain_kernel,
        [((2, 2, CORE, width), f32)] * 2 + [((NODES // 4, first.shape[1]), bf16) for first in firsts],
        (place, inner_model, after(outer_model, recur), gain, *firsts),
        micros=1.0,
        name="gain",
    )
    total = pairs * 2 * tiles
    seconds = [lax.ppermute(quarter, "row", [(i, i ^ 1) for i in range(bands)]) for quarter in quarters]
    weight_own = after(input_weight, gained_same, *seconds)
    parts = call(
        functools.partial(drive_kernel, pairs),
        [((8 * 2 * tiles, NODES), bf16)] * pairs,
        (place, *patches, weight_own, weight_other, recur),
        [
            pltpu.VMEM((message[0] * total * message[2], LANES), f32),
            pltpu.VMEM((2, 4 * total, -(-depth // 2 * PATCH // LANES) * LANES), bf16),
        ],
        10,
        4.0,
        name="drive",
    )
    parts = [along(part, ahead) for ahead, part in enumerate(parts)]
    for first, second in zip(firsts, seconds):
        readout_weights += [first, second, across(after(first, parts[0])), across(after(second, parts[0]))]

    fresh_same, fresh_away, own_same, own_away, far_same, far_away = call(
        functools.partial(readout_kernel, pairs),
        [((2, 2 * tiles, NODES), f32)] * 2 + [((CORE, 2 * tiles, LANES), bf16)] * 4,
        (place, *parts, *readout_weights),
        megabytes=12,
        micros=2.5,
        name="readout",
    )
    pattern = [(i, ((i + sections // 2) % sections) ^ 1) for i in range(sections)]
    far_same = along(far_same, pairs // 2)
    far_away = lax.ppermute(far_away, "col", pattern)
    own_away = across(own_away)
    fresh_away = across(fresh_away)
    gained_away = across(after(gained_away, own_same))
    return call(
        final_kernel,
        [((2, height, width), f32), ((block_rows, 2 * tiles, NODES), f32)],
        (place, own_same, own_away, far_same, far_away, gained_same, gained_away, fresh_same, fresh_away),
        [pltpu.VMEM((CORE * 2 * tiles, LANES), f32)],
        4,
        2.0,
        name="final",
    )


def solution(mesh):
    placed = (
        P(None, "row", "col"),
        P("row", "col", None),
        P("col", None),
        P(),
        P(),
        P(None, "col"),
        P(),
    )
    return jax.shard_map(
        local,
        mesh=mesh,
        in_specs=placed,
        out_specs=(P(None, "row", "col"), P("row", "col", None)),
        check_vma=False,
    )
```

```python
import functools

import jax
import jax.numpy as jnp
from jax import lax
from jax.experimental import pallas as pl
from jax.experimental.pallas import tpu as pltpu
from jax.sharding import PartitionSpec as P

CORE = 64
MARGIN = 4
NODES = 512
PATCH = 72
LANES = 128
STAGES = 4
GROUP = 8
REACH = MARGIN + STAGES
WINDOW = CORE + 2 * REACH

dispersion = 2.0
nonlinear = -0.7
time_step = 0.1

bf16 = jnp.bfloat16
f32 = jnp.float32
VMEM = pl.BlockSpec(memory_space=pltpu.VMEM)
SMEM = pl.BlockSpec(memory_space=pltpu.SMEM)


def call(kernel, outs, operands, scratch=(), megabytes=4, micros=1.0, name=None):
    return pl.pallas_call(
        kernel,
        out_shape=tuple(jax.ShapeDtypeStruct(*out) for out in outs),
        in_specs=[SMEM] + [VMEM] * (len(operands) - 1),
        out_specs=tuple(VMEM for _ in outs),
        scratch_shapes=list(scratch),
        compiler_params=pltpu.CompilerParams(vmem_limit_bytes=megabytes * 2**20),
        cost_estimate=pl.CostEstimate(flops=0, bytes_accessed=int(micros * 3.69e6), transcendentals=0),
        name=name,
    )(*operands)


def tendency(real_part, imag_part):
    def spread(values):
        rows, cols = values.shape
        return (
            pltpu.roll(values, 1, 0)
            + pltpu.roll(values, rows - 1, 0)
            + pltpu.roll(values, 1, 1)
            + pltpu.roll(values, cols - 1, 1)
            - 4.0 * values
        )

    real_spread = spread(real_part)
    imag_spread = spread(imag_part)
    modulus = real_part * real_part + imag_part * imag_part
    first = (
        real_part
        + real_spread
        - dispersion * imag_spread
        - modulus * (real_part - nonlinear * imag_part)
    )
    second = (
        imag_part
        + imag_spread
        + dispersion * real_spread
        - modulus * (imag_part + nonlinear * real_part)
    )
    return first, second


def forecast(start):
    slope = tendency(*start)
    total = slope
    for ahead, weight in ((0.5, 2.0), (0.5, 2.0), (1.0, 1.0)):
        at = tuple(s + ahead * time_step * k for s, k in zip(start, slope))
        slope = tendency(*at)
        total = tuple(t + weight * k for t, k in zip(total, slope))
    return tuple(s + time_step / 6.0 * t for s, t in zip(start, total))


def aligned(value):
    return pl.multiple_of(value, GROUP)


def both_cores(half, own, other):
    low = jnp.where(half == 0, own, other)
    high = jnp.where(half == 0, other, own)
    return low, high


def tile_of(values, tile):
    return values[:, tile * LANES : (tile + 1) * LANES]


def edges_kernel(place_ref, field_ref, out_ref):
    height, width = field_ref.shape[1:]
    lane = lax.broadcasted_iota(jnp.int32, (GROUP, LANES), 1)
    for channel in range(2):
        packed = None
        for group in range(height // GROUP):
            rows = slice(group * GROUP, (group + 1) * GROUP)
            left = pltpu.roll(field_ref[channel, rows, :LANES], group * STAGES, 1)
            right = pltpu.roll(field_ref[channel, rows, width - LANES :], (group + 1) * STAGES % LANES, 1)
            values = jnp.where(place_ref[0] == 0, left, right)
            packed = values if packed is None else jnp.where(lane >= group * STAGES, values, packed)
        out_ref[channel] = packed


def ends_kernel(place_ref, field_ref, other_ref, outer_ref, outer_other_ref, side_ref, out_ref):
    half = place_ref[0]
    height, width = field_ref.shape[1:]
    lane = lax.broadcasted_iota(jnp.int32, (GROUP, LANES), 1)
    at = aligned((height - REACH) * half)
    for channel in range(2):
        left, right = both_cores(half, outer_ref[channel], outer_other_ref[channel])
        for group in range(height // GROUP):
            after = pltpu.roll(right, (LANES - group * STAGES) % LANES, 1)
            before = pltpu.roll(left, (LANES - (group + 1) * STAGES) % LANES, 1)
            side_ref[channel, group * GROUP : (group + 1) * GROUP, :] = jnp.where(lane < LANES // 2, after, before)
        low, high = both_cores(half, field_ref[channel, pl.ds(at, REACH), :], other_ref[channel, pl.ds(at, REACH), :])
        out_ref[channel, :, :width] = low
        out_ref[channel, :, width : 2 * width] = high
        out_ref[channel, :, 2 * width :] = side_ref[channel, pl.ds(at, REACH), :]


def upper_first(half, row):
    return half if row else 1 - half


def model_kernel(outer, place_ref, field_ref, other_ref, side_ref, *refs):
    if outer:
        ends_ref, inner_ref, *message_refs, model_ref, lines_ref, window_ref = refs
    else:
        lines_ref, model_ref = refs
    half = place_ref[0]
    height, width = field_ref.shape[1:]
    tiles = 2 * width // LANES
    length = WINDOW - REACH if outer else WINDOW
    at = aligned((height - length) * half) if outer else aligned(height // 2 - CORE - REACH + CORE * half)
    start = []
    for channel in range(2):
        own = field_ref[channel, pl.ds(at, length), :]
        other = other_ref[channel, pl.ds(at, length), :]
        cells = jnp.concatenate(both_cores(half, own, other) + (side_ref[channel, pl.ds(at, length), :],), 1)
        if outer:
            window_ref[channel, pl.ds(aligned(REACH * (1 - half)), length), :] = cells
            window_ref[channel, pl.ds(aligned(length * half), REACH), :] = ends_ref[channel]
            cells = window_ref[channel]
        start.append(cells)
    model = forecast(start)
    depth = lines_ref.shape[2]
    for channel, values in enumerate(tuple(start) + model):
        for tile in range(tiles):
            for part in range(PATCH // depth):
                at = MARGIN + part * depth
                lines_ref[channel * (PATCH // depth) + part, tile] = tile_of(values, tile)[at : at + depth].astype(bf16)
    for channel in range(2):
        model_ref[channel] = model[channel][REACH : REACH + CORE, : 2 * width]
    if outer:
        pairs = len(message_refs)
        for ahead, message_ref in enumerate(message_refs):
            of = lax.rem(place_ref[1] + ahead, pairs)
            for row, source_ref in enumerate((inner_ref, lines_ref)):
                if message_ref.shape[0] == 1:
                    at = pl.multiple_of(CORE * upper_first(half, row), CORE)
                    message_ref[0, :, pl.ds(at, PATCH), :] = source_ref[of]
                else:
                    message_ref[row] = source_ref[of]


def gain_kernel(place_ref, inner_ref, outer_ref, gain_ref, *refs):
    count = len(refs) // 2 - 1
    first_refs, (same_ref, away_ref), quarter_refs = refs[:count], refs[count : count + 2], refs[count + 2 :]
    for first_ref, quarter_ref in zip(first_refs, quarter_refs):
        rows = quarter_ref.shape[0]
        begin = pl.multiple_of(place_ref[4] * (first_ref.shape[0] - rows), rows)
        quarter_ref[...] = first_ref[pl.ds(begin, rows), :]
    half = place_ref[0]
    width = same_ref.shape[3]
    for channel in range(2):
        gain = gain_ref[channel]
        for row, model_ref in enumerate((inner_ref, outer_ref)):
            for tile in range(width // LANES):
                lanes = slice(tile * LANES, (tile + 1) * LANES)
                low = model_ref[channel, :, lanes]
                high = model_ref[channel, :, width + tile * LANES : width + (tile + 1) * LANES]
                same_ref[channel, row, :, lanes] = gain * jnp.where(half == 0, low, high)
                away_ref[channel, row, :, lanes] = gain * jnp.where(half == 0, high, low)


def drive_kernel(pairs, place_ref, *refs):
    patch_refs, weight_refs, recur_ref = refs[:pairs], refs[pairs : pairs + 2], refs[pairs + 2]
    out_refs, (cells_ref, left_ref) = refs[pairs + 3 : -2], refs[-2:]
    kinds, tiles, stride, _ = patch_refs[0].shape
    depth = PATCH if kinds == 1 else stride
    total = pairs * tiles
    for row in range(kinds):
        for pair in range(pairs):
            for tile in range(tiles):
                at = (row * total + pair * tiles + tile) * stride
                cells_ref[at : at + stride, :] = patch_refs[pair][row, tile].astype(f32)
    lane = lax.broadcasted_iota(jnp.int32, (total, LANES), 1)
    half = place_ref[0]
    lines = depth // 2
    width = lines * PATCH
    sums = None
    for which in range(2):
        begin = lines * (half if which == 0 else 1 - half)
        for row in range(2):
            held = [None, None]
            for line in range(lines):
                at = CORE * upper_first(half, row) if kinds == 1 else row * total * depth
                own = cells_ref[pl.ds(at + begin + line, total, stride=stride), :]
                before = pltpu.roll(own, 1, 0)
                after = pltpu.roll(own, total - 1, 0)
                even = jnp.where(lane >= LANES - MARGIN, before, own)
                odd = jnp.where(lane < MARGIN, after, own)
                first = line * PATCH
                offset = first % LANES
                lanes = slice(first - offset, first - offset + LANES)
                for parity, (values, shift) in enumerate(((even, MARGIN), (odd, MARGIN + CORE))):
                    at = (row * 2 + parity) * total
                    moved = pltpu.roll(values, (first + shift) % LANES, 1)
                    current = moved if offset == 0 else jnp.where(lane >= offset, moved, held[parity])
                    if offset + PATCH >= LANES or line == lines - 1:
                        left_ref[which, at : at + total, lanes] = current.astype(bf16)
                        if line == lines - 1 and offset + PATCH > LANES:
                            more = slice(lanes.stop, lanes.stop + LANES)
                            left_ref[which, at : at + total, more] = moved.astype(bf16)
                        current = moved
                    held[parity] = current
        term = jnp.dot(left_ref[which, :, :width], weight_refs[which][...], preferred_element_type=f32)
        sums = term if sums is None else sums + term
    for pair, out_ref in enumerate(out_refs):
        pieces = []
        for of in (pair, (pair + pairs // 2) % pairs):
            for part in range(4):
                at = part * total + of * tiles
                piece = sums[at : at + tiles]
                if of == 0:
                    piece = piece + recur_ref[part * tiles : (part + 1) * tiles, :]
                pieces.append(piece)
        out_ref[...] = jnp.concatenate(pieces, 0).astype(bf16)


def part_kernel(place_ref, weight_ref, out_ref, done):
    rows = out_ref.shape[0]
    begin = pl.multiple_of(place_ref[4] * (weight_ref.shape[0] - rows), LANES)
    copy = pltpu.make_async_copy(weight_ref.at[pl.ds(begin, rows), :], out_ref, done)
    copy.start()
    copy.wait()


def row_part(place, weight):
    rows, columns = weight.shape
    return pl.pallas_call(
        part_kernel,
        out_shape=jax.ShapeDtypeStruct((rows - rows // 4, columns), weight.dtype),
        in_specs=[SMEM, pl.BlockSpec(memory_space=pltpu.HBM)],
        out_specs=VMEM,
        scratch_shapes=[pltpu.SemaphoreType.DMA(())],
        compiler_params=pltpu.CompilerParams(vmem_limit_bytes=4 * 2**20),
        cost_estimate=pl.CostEstimate(flops=0, bytes_accessed=2_000_000, transcendentals=0),
        name="part",
    )(place, weight)


def previous_kernel(place_ref, states_ref, same_ref, away_ref):
    half = place_ref[0]
    block_rows, block_cols = states_ref.shape[:2]
    for away, out_ref in enumerate((same_ref, away_ref)):
        of = half if away == 0 else 1 - half
        pieces = []
        for row in (block_rows // 2 - 1 + of, (block_rows - 1) * of):
            values = states_ref[row]
            for parity in range(2):
                pieces += [values[column : column + 1] for column in range(parity, block_cols, 2)]
        out_ref[...] = jnp.concatenate(pieces, 0)


def recur_kernel(place_ref, same_ref, away_ref, weight_ref, bias_ref, out_ref):
    low, high = both_cores(place_ref[0], same_ref[...], away_ref[...])
    tiles = low.shape[0] // 4
    pieces = []
    for index in range(4):
        pieces += [values[index * tiles : (index + 1) * tiles] for values in (low, high)]
    previous = jnp.concatenate(pieces, 0).astype(bf16)
    out_ref[...] = jnp.dot(previous, weight_ref[...], preferred_element_type=f32) + bias_ref[...]


def halves(half, first, second):
    rows = first.shape[0]
    row = lax.broadcasted_iota(jnp.int32, first.shape, 0)
    low = jnp.where(row < rows // 2, first, pltpu.roll(second, rows // 2, 0))
    high = jnp.where(row < rows // 2, pltpu.roll(first, rows // 2, 0), second)
    return jnp.where(half == 0, low, high), jnp.where(half == 0, high, low)


def readout_kernel(pairs, place_ref, *refs):
    parts, weights = refs[:pairs], refs[pairs:-6]
    fresh_same, fresh_away, own_same, own_away, far_same, far_away = refs[-6:]
    half = place_ref[0]
    total = sum(part[...].astype(f32) for part in parts)
    fresh = jnp.tanh(total)
    tiles = fresh.shape[0] // 8
    for row in range(2):
        at = row * 2 * tiles
        same, away = halves(half, fresh[at : at + tiles], fresh[at + tiles : at + 2 * tiles])
        fresh_same[row] = same
        fresh_away[row] = away
    readin = fresh.astype(bf16)
    lane = lax.broadcasted_iota(jnp.int32, (tiles, LANES), 1)
    odd = place_ref[4] == 1
    quarter = NODES // 4
    most = jnp.where(odd, readin[:, quarter:], readin[:, : NODES - quarter])
    rest = jnp.where(odd, readin[:, :quarter], readin[:, NODES - quarter :])
    for index in range(len(weights) // 2 + 1):
        if index < 2:
            products = jnp.dot(readin, weights[index][...], preferred_element_type=f32)
        else:
            head, tail = weights[2 * index - 2 : 2 * index]
            products = jnp.dot(most, head[...], preferred_element_type=f32)
            products = products + jnp.dot(rest, tail[...], preferred_element_type=f32)
        lines = products.shape[1] // CORE
        begin = lax.bitwise_xor(place_ref[2], index) * lines
        for tile in range(products.shape[1] // LANES):
            values = tile_of(products, tile)
            for of, (same_ref, away_ref) in enumerate(((own_same, own_away), (far_same, far_away))):
                pair = []
                for row in range(2):
                    at = (of * 2 + row) * 2 * tiles
                    low, high = values[at : at + tiles], values[at + tiles : at + 2 * tiles]
                    pair.append(
                        (
                            jnp.where(lane < CORE, low, pltpu.roll(high, CORE, 1)),
                            jnp.where(lane < CORE, pltpu.roll(low, CORE, 1), high),
                        )
                    )
                for line in range(2):
                    same, away = halves(half, pair[0][line], pair[1][line])
                    same_ref[begin + 2 * tile + line] = same.astype(bf16)
                    away_ref[begin + 2 * tile + line] = away.astype(bf16)


def own_kernel(place_ref, own_same, own_away, gained_same, gained_away, out_ref, cells_ref):
    side = place_ref[3]
    tiles = out_ref.shape[2] // LANES
    rows = 2 * tiles
    for away, (own, gained) in enumerate(((own_same, gained_same), (own_away, gained_away))):
        cells_ref[...] = own[...].astype(f32).reshape(CORE * rows, LANES)
        for row in range(2):
            for tile in range(tiles):
                lanes = slice(tile * LANES, (tile + 1) * LANES)
                placed = cells_ref[pl.ds(row * tiles + tile, CORE, stride=rows), :]
                out_ref[away * 2 + row, :, lanes] = gained[side, row, :, lanes] + placed


def final_kernel(
    place_ref,
    own_sums,
    far_same,
    far_away,
    gained_same,
    gained_away,
    fresh_same,
    fresh_away,
    out_ref,
    states_ref,
    cells_ref,
):
    half = place_ref[0]
    side = place_ref[3]
    tiles = out_ref.shape[2] // LANES
    block_rows = out_ref.shape[1] // CORE
    rows = 2 * tiles
    for away, (far, gained, fresh) in enumerate(
        ((far_same, gained_same, fresh_same), (far_away, gained_away, fresh_away))
    ):
        of = half if away == 0 else 1 - half
        places = (block_rows // 2 - 1 + of, (block_rows - 1) * of)
        cells_ref[...] = far[...].astype(f32).reshape(CORE * rows, LANES)
        for row in range(2):
            at = pl.multiple_of(places[row] * CORE, CORE)
            out_ref[side, pl.ds(at, CORE), :] = own_sums[away * 2 + row]
            for tile in range(tiles):
                lanes = slice(tile * LANES, (tile + 1) * LANES)
                placed = cells_ref[pl.ds(row * tiles + tile, CORE, stride=rows), :]
                out_ref[1 - side, pl.ds(at, CORE), lanes] = gained[1 - side, row, :, lanes] + placed
        for row in range(2):
            for column in range(2 * tiles):
                at = (column % 2) * tiles + column // 2
                states_ref[places[row], column : column + 1, :] = fresh[row, at : at + 1, :]


def after(values, *others):
    return lax.optimization_barrier((values,) + others)[0]


def local(field, states, input_weight, recurrent_weight, bias, output_weight, model_gain):
    height, width = field.shape[1:]
    sections = lax.axis_size("col")
    bands = lax.axis_size("row")
    pairs = sections // 2
    block_rows = height // CORE
    tiles = width // LANES
    depth = 4 * PATCH // pairs
    slices = sections // 2
    column = lax.axis_index("col")
    band = lax.axis_index("row")
    half = column % 2
    place = jnp.stack([half, column // 2, column % slices, column // slices, band % 2])

    def across(values):
        return lax.ppermute(values, "col", [(i, i ^ 1) for i in range(sections)])

    def along(values, ahead):
        if ahead % pairs == 0:
            return values
        return lax.ppermute(values, "col", [(i, (i + 2 * ahead) % sections) for i in range(sections)])

    other = across(field)
    (edges,) = call(edges_kernel, [((2, GROUP, LANES), f32)], (place, field), name="edges")
    pattern = [(i, (i + (1 if i % 2 else -1)) % sections) for i in range(sections)]
    edges = lax.ppermute(edges, "col", pattern)
    edges_other = across(after(edges, other))
    side, ends = call(
        ends_kernel,
        [((2, height, LANES), f32), ((2, REACH, 2 * width + LANES), f32)],
        (place, field, other, edges, edges_other),
        name="ends",
    )
    pattern = []
    for item in range(bands):
        for core in range(0, sections, 2):
            pattern.append((item * sections + core, (item - 1) % bands * sections + core + 1))
            pattern.append((item * sections + core + 1, (item + 1) % bands * sections + core))
    ends = lax.ppermute(ends, ("row", "col"), pattern)

    weight_other = across(after(input_weight, edges_other))
    readout_weights = [output_weight, across(after(output_weight, edges_other))]
    part = row_part(place, after(output_weight, side))
    patterns = [[(i, i ^ index) for i in range(sections)] for index in range(2, slices, 2)]
    firsts = [lax.ppermute(part, "col", pattern) for pattern in patterns]

    lines = ((pairs, 2 * tiles, depth, LANES), bf16)
    model = ((2, CORE, 2 * width), f32)
    message = (1, 2 * tiles, PATCH + CORE, LANES) if depth == PATCH else (2, 2 * tiles, depth, LANES)
    inner_lines, inner_model = call(
        functools.partial(model_kernel, False),
        [lines, model],
        (place, field, other, side),
        megabytes=8,
        micros=3.3,
        name="inner_model",
    )
    *messages, outer_model = call(
        functools.partial(model_kernel, True),
        [(message, bf16)] * pairs + [model],
        (place, field, other, side, after(ends, inner_model, weight_other, readout_weights[1]), inner_lines),
        [pltpu.VMEM(*lines), pltpu.VMEM((2, WINDOW, 2 * width + LANES), f32)],
        12,
        3.3,
        name="outer_model",
    )
    patches = [along(messages[-ahead % pairs], -ahead) for ahead in range(pairs)]
    previous = call(
        previous_kernel,
        [((block_rows * tiles, NODES), f32)] * 2,
        (place, after(states, outer_model)),
        micros=0.5,
        name="previous",
    )
    (recur,) = call(
        recur_kernel,
        [((2 * block_rows * tiles, NODES), f32)],
        (place, previous[0], across(previous[1]), recurrent_weight, bias[None]),
        micros=0.5,
        name="recur",
    )

    gain = jnp.concatenate([model_gain, model_gain], 2)
    gained_same, gained_away, *quarters = call(
        gain_kernel,
        [((2, 2, CORE, width), f32)] * 2 + [((NODES // 4, first.shape[1]), bf16) for first in firsts],
        (place, inner_model, after(outer_model, recur), gain, *firsts),
        micros=1.0,
        name="gain",
    )
    total = pairs * 2 * tiles
    seconds = [lax.ppermute(quarter, "row", [(i, i ^ 1) for i in range(bands)]) for quarter in quarters]
    weight_own = after(input_weight, gained_same, *seconds)
    parts = call(
        functools.partial(drive_kernel, pairs),
        [((8 * 2 * tiles, NODES), bf16)] * pairs,
        (place, *patches, weight_own, weight_other, recur),
        [
            pltpu.VMEM((message[0] * total * message[2], LANES), f32),
            pltpu.VMEM((2, 4 * total, -(-depth // 2 * PATCH // LANES) * LANES), bf16),
        ],
        10,
        4.0,
        name="drive",
    )
    parts = [along(part, ahead) for ahead, part in enumerate(parts)]
    for first, second in zip(firsts, seconds):
        readout_weights += [first, second, across(after(first, parts[0])), across(after(second, parts[0]))]

    fresh_same, fresh_away, own_same, own_away, far_same, far_away = call(
        functools.partial(readout_kernel, pairs),
        [((2, 2 * tiles, NODES), f32)] * 2 + [((CORE, 2 * tiles, LANES), bf16)] * 4,
        (place, *parts, *readout_weights),
        megabytes=12,
        micros=2.5,
        name="readout",
    )
    pattern = [(i, ((i + sections // 2) % sections) ^ 1) for i in range(sections)]
    far_same = along(far_same, pairs // 2)
    far_away = lax.ppermute(far_away, "col", pattern)
    own_away = across(own_away)
    fresh_away = across(fresh_away)
    gained_away = across(after(gained_away, own_same))
    (own_sums,) = call(
        own_kernel,
        [((4, CORE, width), f32)],
        (place, own_same, own_away, gained_same, gained_away),
        [pltpu.VMEM((CORE * 2 * tiles, LANES), f32)],
        name="own",
    )
    return call(
        final_kernel,
        [((2, height, width), f32), ((block_rows, 2 * tiles, NODES), f32)],
        (place, own_sums, far_same, far_away, gained_same, gained_away, fresh_same, fresh_away),
        [pltpu.VMEM((CORE * 2 * tiles, LANES), f32)],
        4,
        2.0,
        name="final",
    )


def solution(mesh):
    placed = (
        P(None, "row", "col"),
        P("row", "col", None),
        P("col", None),
        P(),
        P(),
        P(None, "col"),
        P(),
    )
    return jax.shard_map(
        local,
        mesh=mesh,
        in_specs=placed,
        out_specs=(P(None, "row", "col"), P("row", "col", None)),
        check_vma=False,
    )
```
